32 devices in a mesh: dev: 32 (over z, y, x, core).
Axes of the slice: x: 2, y: 2, z: 4, core: 2. Of those that a mesh axis runs over, the one named last changes fastest.
Arguments:
- params: float32 [9, 32768], P(None, 'dev')
- moment: float32 [9, 32768], P(None, 'dev'), may hold values from -3 to 3
- second: float32 [9, 32768], P(None, 'dev'), may hold values from 0.05 to 1
- fetch_ids: int32 [32, 32, 8], P('dev'), may hold values from 0 to 1023
- seg_ids: int32 [128, 256], P('dev'), may hold values from 0 to 255
- seg_count: int32 [128], P('dev'), may hold values from 1 to 256, 24576 in all
- seg_perm: int32 [128], replicated, may hold values from 0 to 127, as said below
- target: float32 [32, 3, 256], P('dev'), may hold values from 0 to 1
Outputs:
- image: float32 [32, 3, 256], P('dev')
- new_params: float32 [9, 32768], P(None, 'dev')
- new_moment: float32 [9, 32768], P(None, 'dev')
- new_second: float32 [9, 32768], P(None, 'dev')
The draws below stay inside these ranges and needn't reach their ends.
Inputs may be any that keep to these rules, and one draw needn't show every extreme that they name: `seg_count`: segments that exceed their count hold unused slots; some segment is full. `seg_perm`: each number appears once.
All inputs are finite; a program needn't handle non-finite values. No bound on the sum of `seg_count` on one device may be relied on, other than what follows from the above.
Results may differ from the reference program's by a relative error of at most 0.0003.
Values sent between devices are 32-bit elements; how exact they have to be, the bound alone decides.
No kernel may reach another device: no remote copies, remote signals or barrier semaphores. Data moves between devices by JAX's collectives and lax.ppermute only.
A program may use at most 192 MiB of HBM per device.

```python
import math
import jax
import jax.numpy as jnp
import numpy as np
from jax import lax

PARAMS = 9
TILE_PIX = 256
TILES_X = 8
KSEG = 4
SEG_LEN = 256
SPL_DEV = 1024
CAP = 8
SEGS_DEV = 4
SPLATS = 32768
SLOTS = 256
SEGMENTS = 128
TILES = 32
N_DEV = 32


def permute_rows(key, rows, width):
    return jax.vmap(lambda one: jax.random.permutation(one, width))(jax.random.split(key, rows)).astype(jnp.int32)


def layout(key):
    base = jax.random.fold_in(key, 101)
    seg_perm = jax.random.permutation(jax.random.fold_in(base, 1), SEGMENTS).astype(jnp.int32)
    orders = permute_rows(jax.random.fold_in(base, 2), N_DEV, SPL_DEV)
    request = jnp.arange(N_DEV, dtype=jnp.int32)[:, None, None] * CAP + jnp.arange(CAP, dtype=jnp.int32)[None, None, :]
    request = jnp.broadcast_to(request, (N_DEV, N_DEV, CAP)) % SPL_DEV
    owners = jnp.broadcast_to(jnp.arange(N_DEV, dtype=jnp.int32)[None, :, None], (N_DEV, N_DEV, CAP))
    fresh = orders[owners, request]
    repeat = jax.random.randint(jax.random.fold_in(base, 3), (N_DEV, N_DEV, CAP), 0, 8) == 0
    partner = jax.random.randint(jax.random.fold_in(base, 4), (N_DEV, N_DEV, CAP), 0, CAP).astype(jnp.int32)
    within = jnp.broadcast_to(jnp.arange(CAP, dtype=jnp.int32), (N_DEV, N_DEV, CAP))
    source = jnp.where(repeat, partner, within)
    fetch_ids = jnp.take_along_axis(fresh, source, axis=2).astype(jnp.int32)
    home_base = (permute_rows(jax.random.fold_in(base, 5), N_DEV, SLOTS) % SEGS_DEV).reshape(N_DEV, N_DEV, CAP)
    home = jnp.take_along_axis(home_base, source, axis=2).reshape(N_DEV, SLOTS).astype(jnp.int32)
    tiebreak = permute_rows(jax.random.fold_in(base, 6), N_DEV, SLOTS)
    sorted_slots = jnp.argsort(home * SLOTS + tiebreak, axis=1).astype(jnp.int32)
    counts = jnp.sum((home[:, None, :] == jnp.arange(SEGS_DEV, dtype=jnp.int32)[None, :, None]).astype(jnp.int32), axis=2).astype(jnp.int32)
    starts = jnp.cumsum(counts, axis=1).astype(jnp.int32) - counts
    picks = jax.random.randint(jax.random.fold_in(base, 7), (N_DEV, SEGS_DEV, SEG_LEN), 0, 1 << 30).astype(jnp.int32)
    position = starts[:, :, None] + picks % jnp.maximum(counts, 1)[:, :, None]
    position = jnp.minimum(position, SLOTS - 1).reshape(N_DEV, SEGS_DEV * SEG_LEN)
    chosen = jnp.take_along_axis(sorted_slots, position, axis=1).reshape(N_DEV, SEGS_DEV, SEG_LEN)
    seg_ids = jnp.where(counts[:, :, None] > 0, chosen, picks % SLOTS).reshape(SEGMENTS, SEG_LEN).astype(jnp.int32)
    device_base = jnp.arange(N_DEV, dtype=jnp.int32)[:, None] * SEGS_DEV
    slot_tile = seg_perm[device_base + home] // KSEG
    global_ids = (jnp.arange(N_DEV, dtype=jnp.int32)[None, :, None] * SPL_DEV + fetch_ids).reshape(N_DEV, SLOTS)
    score = jnp.arange(N_DEV, dtype=jnp.int32)[:, None] * SLOTS + jnp.arange(SLOTS, dtype=jnp.int32)[None, :]
    user = jnp.full((SPLATS,), -1, jnp.int32).at[global_ids.reshape(-1)].max(score.reshape(-1))
    spare = jax.random.randint(jax.random.fold_in(base, 8), (SPLATS,), 0, TILES).astype(jnp.int32)
    splat_tile = jnp.where(user >= 0, slot_tile.reshape(-1)[jnp.maximum(user, 0)], spare).astype(jnp.int32)
    return (fetch_ids, seg_ids, seg_perm, splat_tile)


def draw_fetch_ids(key, part):
    return layout(key)[0]


def draw_seg_ids(key, part):
    return layout(key)[1]


def draw_seg_perm(key, part):
    return layout(key)[2]


def draw_params(key, part):
    splat_tile = layout(key)[3]
    keys = jax.random.split(jax.random.fold_in(key, 11), 10)
    count = SPLATS
    scales = jax.random.uniform(keys[2], (2, count), jnp.float32, 1.5, 3.0)
    sigma_x = jnp.exp(-scales[0])
    sigma_y = jnp.exp(-scales[1])
    corner_x = (splat_tile % TILES_X).astype(jnp.float32)
    corner_y = (splat_tile // TILES_X).astype(jnp.float32)
    centre_x = corner_x + jax.random.uniform(keys[0], (count,), jnp.float32, 0.0, 1.0) + 2.0 * sigma_x * jax.random.uniform(keys[6], (count,), jnp.float32, -1.0, 1.0)
    centre_y = corner_y + jax.random.uniform(keys[1], (count,), jnp.float32, 0.0, 1.0) + 2.0 * sigma_y * jax.random.uniform(keys[7], (count,), jnp.float32, -1.0, 1.0)
    opaque = jax.random.uniform(keys[8], (count,), jnp.float32, 0.0, 1.0) < min(1.0, 16.0 / SEG_LEN)
    weak = jax.random.uniform(keys[9], (count,), jnp.float32, -8.0, -1.0)
    tilt = jax.random.normal(keys[3], (1, count), jnp.float32)
    strong = jax.random.uniform(keys[4], (count,), jnp.float32, 1.0, 4.0)
    colours = jax.random.uniform(keys[5], (3, count), jnp.float32, 0.0, 1.0)
    opacity = jnp.where(opaque, strong, weak)[None, :]
    return jnp.concatenate([centre_x[None, :], centre_y[None, :], scales, tilt, opacity, colours], axis=0)


def block_levels(stream_key, extent, pieces, smallest, top_value):
    level = 1.0
    for dim, blocks in pieces:
        steps = jax.random.uniform(jax.random.fold_in(jax.random.fold_in(stream_key, 6), dim), (blocks,), jnp.float32, smallest / len(pieces), top_value / len(pieces))
        level = level * jnp.repeat(jnp.exp(steps), extent[dim] // blocks).reshape((-1,) + (1,) * (len(extent) - 1 - dim))
    return level


def length_profile(amount, total, reach, slope):
    weights = [(1 << 20) // math.isqrt(standing ** slope) + 1 for standing in range(2, amount + 1)]
    surplus, given = total - reach - (amount - 1), [1] * (amount - 1)
    while surplus > 0:
        free = [i for i in range(amount - 1) if given[i] < reach]
        mass, remaining = sum([weights[i] for i in free]), surplus
        for i in free:
            more = min(reach - given[i], max(1, remaining * weights[i] // mass), surplus)
            given[i] = given[i] + more
            surplus = surplus - more
    return np.array([reach] + given)


def ragged(own_key, number_of, total, limit, skew):
    if number_of == 2:
        one = jax.random.randint(own_key, (), max(1, total - limit), min(limit, total - 1) + 1)
        return jnp.stack([one, total - one])
    lengths = jnp.asarray(length_profile(number_of, total, limit, skew), jnp.int32)
    couples = (number_of - 1) // 2
    giver, receiver = lengths[1:1 + 2 * couples:2], lengths[2:2 + 2 * couples:2]
    room = jnp.minimum(giver - 1, limit - receiver)
    moved = jax.random.randint(jax.random.fold_in(own_key, 1), (couples,), 0, 1 << 20) % (room + 1)
    lengths = lengths.at[1:1 + 2 * couples:2].set(giver - moved).at[2:2 + 2 * couples:2].set(receiver + moved)
    return lengths[jax.random.permutation(jax.random.fold_in(own_key, 2), number_of)]


def gaussian(key, extent, spread, limit, cuts=(), kind=jnp.bfloat16):
    gain = block_levels(key, extent, cuts, -0.22, 0.18) if cuts else 1.0
    array = jax.random.normal(key, extent, jnp.float32) * spread * gain
    return jnp.minimum(jnp.maximum(array, -limit), limit).astype(kind)


def setup_inputs(seed: int = 0) -> dict:
    key_list = jax.random.split(jax.random.key(seed), 9)
    params = draw_params(jax.random.fold_in(key_list[8], 71), 0)
    moment = gaussian(key_list[1], (PARAMS, SPLATS), 0.5, 3.0, ((1, 32),), jnp.float32)
    second = jnp.clip(jnp.exp(math.log(1.0) - 2.9957323 * jax.random.uniform(key_list[2], (PARAMS, SPLATS), jnp.float32) ** block_levels(key_list[2], (PARAMS, SPLATS), ((1, 32),), -0.2, 0.2)), 0.05, 1.0)
    fetch_ids = draw_fetch_ids(jax.random.fold_in(key_list[8], 71), 0)
    seg_ids = draw_seg_ids(jax.random.fold_in(key_list[8], 71), 0)
    seg_count = ragged(key_list[5], SEGMENTS, SEGMENTS * SEG_LEN * 3 // 4, SEG_LEN, 2).astype(jnp.int32)
    seg_perm = draw_seg_perm(jax.random.fold_in(key_list[8], 71), 0)
    target = jnp.clip(1.0 * jax.random.uniform(key_list[7], (TILES, 3, TILE_PIX), jnp.float32) ** block_levels(key_list[7], (TILES, 3, TILE_PIX), ((0, 32),), -0.2, 0.2), 0.0, 1.0)
    return {"params": params, "moment": moment, "second": second, "fetch_ids": fetch_ids, "seg_ids": seg_ids, "seg_count": seg_count, "seg_perm": seg_perm, "target": target}


def segment(par, count, tile):
    span = par.shape[1]
    pidx = jnp.arange(256, dtype=jnp.int32)
    fine_x = ((pidx % 16).astype(jnp.float32) + 0.5) / 16.0
    fine_y = ((pidx // 16).astype(jnp.float32) + 0.5) / 16.0
    pos_x = (tile % TILES_X).astype(jnp.float32) + fine_x
    pos_y = (tile // TILES_X).astype(jnp.float32) + fine_y
    live = (jnp.arange(span, dtype=jnp.int32) < count).astype(jnp.float32)
    delta_x = pos_x[None, :] - par[0][:, None]
    delta_y = pos_y[None, :] - par[1][:, None]
    scale_a = jnp.exp(par[2])
    scale_c = jnp.exp(par[3])
    cross = 0.8 * jnp.tanh(par[4]) * scale_a * scale_c
    power = -0.5 * ((scale_a * scale_a)[:, None] * delta_x * delta_x + 2.0 * cross[:, None] * delta_x * delta_y + (scale_c * scale_c)[:, None] * delta_y * delta_y)
    alpha = (0.95 * jax.nn.sigmoid(par[5]) * live)[:, None] * jnp.exp(power)
    logt = jnp.log1p(-alpha)
    earlier = jnp.cumsum(logt, axis=0) - logt
    weight = jnp.exp(earlier) * alpha
    colour = jnp.dot(par[6:9], weight, precision=lax.Precision.HIGHEST)
    return (colour, lax.optimization_barrier(jnp.sum(logt, axis=0)))

def reference(params, moment, second, fetch_ids, seg_ids, seg_count, seg_perm, target):
    slots = jnp.arange(SEGMENTS, dtype=jnp.int32)
    requester = slots // SEGS_DEV
    owner = seg_ids // CAP
    within = seg_ids % CAP
    local = fetch_ids[requester[:, None], owner, within]
    global_ids = owner * SPL_DEV + local
    tiles = seg_perm // KSEG
    order = jnp.zeros((SEGMENTS,), jnp.int32).at[seg_perm].set(slots)

    def render(values):

        def one(args):
            ids, count, tile = args
            return segment(jnp.take(values, ids, axis=1), count, tile)
        colours, logs = lax.map(jax.checkpoint(one), (global_ids, seg_count, tiles))
        colours = colours[order].reshape(TILES, KSEG, 3, TILE_PIX)
        logs = logs[order].reshape(TILES, KSEG, TILE_PIX)
        before = jnp.cumsum(logs, axis=1) - logs
        return lax.optimization_barrier(jnp.sum(jnp.exp(before)[:, :, None, :] * colours, axis=1))
    image, back = jax.vjp(render, params)
    grad, = back(image - target)
    new_moment = 0.9 * moment + 0.1 * grad
    new_second = 0.99 * second + 0.01 * grad * grad
    new_params = params - 0.05 * new_moment / (jnp.sqrt(new_second) + 1e-08)
    return (image, new_params, new_moment, new_second)
```

```python
import functools

import jax
import jax.numpy as jnp
from jax import lax
from jax.experimental import pallas as pl
from jax.experimental.pallas import tpu as pltpu
from jax.sharding import PartitionSpec as P

TILES_X = 8
KSEG = 4
SIDE = 16
LANES = 128
GROUP = 32
ROWS = 16
F32 = jnp.float32
BF16 = jnp.bfloat16
SMEM = pl.BlockSpec(memory_space=pltpu.SMEM)
VMEM = pl.BlockSpec(memory_space=pltpu.VMEM)
PARAMS = pltpu.CompilerParams(vmem_limit_bytes=40 * 2**20)


def split2(x):
    high = x.astype(BF16)
    return high, (x - high.astype(F32)).astype(BF16)


def split3(x):
    high = x.astype(BF16)
    rest = x - high.astype(F32)
    mid = rest.astype(BF16)
    return high, mid, (rest - mid.astype(F32)).astype(BF16)


def iota(shape, dim):
    return lax.broadcasted_iota(jnp.int32, shape, dim)


def dot(a, b, dims=((1,), (0,))):
    return lax.dot_general(a, b, (dims, ((), ())), preferred_element_type=F32)


def one_hot_rows(ids, cap, width):
    cols = iota((ids.shape[0], width), 1)
    return jnp.concatenate([(ids[:, k : k + 1] == cols).astype(F32).astype(BF16) for k in range(cap)], 0)


def request_kernel(cap, count, seg, fetch, out, moved, base):
    segs, span = seg.shape
    ndev, rows, _ = out.shape
    halves = span // LANES
    lane = iota((1, LANES), 1)
    for s in range(segs):
        for h in range(halves):
            live = lane + h * LANES < count[s]
            row = s * halves + h
            base[row : row + 1, :] = jnp.where(live, seg[s : s + 1, h * LANES : (h + 1) * LANES], -1)
    block = base[...]
    sub, lanes = iota((rows, LANES), 0), iota((rows, LANES), 1)
    slot = (sub == rows - 1) & (lanes < cap)
    for d in range(ndev):
        wide = jnp.broadcast_to(fetch[d : d + 1, :], (rows, LANES))
        out[d] = jnp.where(slot, wide, block)
    last = jnp.broadcast_to(block[rows - 1 : rows, :], (rows, LANES)).astype(F32)
    column = jnp.sum(jnp.where(sub == lanes, last, 0.0), axis=1, keepdims=True)
    moved[...] = jnp.where(lanes == LANES - 1, column, 0.0)


def send_kernel(segs, cap, perm, ids_in, params, moved, out, order, wide, picked):
    ndev, rows, _ = ids_in.shape
    nparam, owned = params.shape
    total = perm.shape[0]

    def place(j, carry):
        order[perm[j]] = j
        return carry

    lax.fori_loop(0, total, place, 0, unroll=8)
    hot = one_hot_rows(ids_in[:, rows - 1, :], cap, owned)
    wide[...] = jnp.zeros(wide.shape, F32)
    for q in range(KSEG):
        wide[q * GROUP : q * GROUP + nparam, :] = params[...]
    picked[...] = sum(dot(hot, part, ((1,), (1,))) for part in split3(wide[...]))
    group = iota((cap, LANES), 1) // GROUP
    extra = moved[...]

    def send(t, carry):
        block = extra
        for q in range(KSEG):
            r = order[t * KSEG + q] // segs
            block = block + jnp.where(group == q, picked[pl.ds(r, cap, stride=ndev), :], 0.0)
        out[t] = block
        return carry

    lax.fori_loop(0, ndev, send, 0, unroll=4)


def render_kernel(
    segs, cap, nparam, me, order, arrived, lists, target, image, grads,
    bufs, hots, coef, ids, alpha, trans, logs, weights, backs, lower, dys, dpar, gback,
):
    ndev, rows, _ = lists.shape
    slots = ndev * cap
    pixels = SIDE * SIDE
    span = hots.shape[2]
    halves = span // LANES
    tile = me[0]
    bufs[...] = arrived[...].reshape(slots, LANES).T
    src, dst = iota((span, span), 0), iota((span, span), 1)
    before = (src < dst).astype(F32).astype(BF16)
    after = (src > dst).astype(F32).astype(BF16)
    lower[0, :span, :] = before
    lower[0, span:, :] = before
    lower[1, :span, :] = after
    lower[1, span:, :] = after
    slot_row = iota((slots, span), 0)
    fine = (iota((SIDE, span), 0).astype(F32) + 0.5) / SIDE
    pos_x = (tile % TILES_X).astype(F32) + fine
    pos_y = (tile // TILES_X).astype(F32) + fine
    sub8, lane8 = iota((cap, LANES), 0), iota((cap, LANES), 1)

    par, dxs, rates = [], [], []
    for q in range(KSEG):
        j = order[tile * KSEG + q]
        r, s = j // segs, j % segs
        tail = jnp.broadcast_to(arrived[r][:, LANES - 1 : LANES], (cap, LANES))
        tail = jnp.sum(jnp.where(sub8 == lane8, tail, 0.0), axis=0, keepdims=True).astype(jnp.int32)
        for h in range(halves):
            row = lists[r, pl.ds(s * halves + h, 1), :]
            if h == halves - 1:
                fix = (iota((1, LANES), 1) < cap) & (s == segs - 1)
                row = jnp.where(fix, tail, row)
            ids[q : q + 1, h * LANES : (h + 1) * LANES] = row
        own = ids[q : q + 1, :]
        hot = (slot_row == own).astype(F32).astype(BF16)
        hots[q] = hot
        parts = jnp.concatenate(split3(bufs[q * GROUP : q * GROUP + ROWS, :]), 0)
        got = dot(parts, hot)
        got = got[:ROWS] + got[ROWS : 2 * ROWS] + got[2 * ROWS :]
        coef[q] = got
        mx, my = got[0:1], got[1:2]
        ex, ey = jnp.exp(got[2:3]), jnp.exp(got[3:4])
        th = jnp.tanh(got[4:5])
        sa, sc, cross = ex * ex, ey * ey, 0.8 * th * ex * ey
        live = (own >= 0).astype(F32)
        peak = 0.95 / (1.0 + jnp.exp(-got[5:6])) * live
        dx = pos_x - mx
        dy = pos_y - my
        xa = -0.5 * sa * dx * dx
        xb = -cross * dx
        dys[q, 0] = dy
        dys[q, 1] = -0.5 * sc * dy * dy
        par.append((sa, sc, cross, ex, ey, th))
        dxs.append(dx)
        for y in range(SIDE):
            power = xa + dys[q, 0, y : y + 1, :] * xb + dys[q, 1, y : y + 1, :]
            al = peak * jnp.exp(power)
            at = slice(y * SIDE, (y + 1) * SIDE)
            alpha[q, at, :] = al
            hi, mid = split2(jnp.log(1.0 - al))
            logs[q, at, :span] = hi
            logs[q, at, span:] = mid
        trans[q] = dot(logs[q], lower[0])

    ahead = jnp.zeros((pixels, 1), F32)
    shown = jnp.zeros((pixels, LANES), F32)
    lane = iota((pixels, LANES), 1)
    for q in range(KSEG):
        front = jnp.broadcast_to(ahead, (pixels, LANES))
        gback[...] = front
        ahead = ahead + trans[q, :, span - 1 : span] + jnp.log(1.0 - alpha[q, :, span - 1 : span])
        for y in range(SIDE):
            at = slice(y * SIDE, (y + 1) * SIDE)
            both = jnp.concatenate([gback[at, :]] * halves, 1)
            t = jnp.exp(trans[q, at, :] + both)
            trans[q, at, :] = t
            hi, mid = split2(t * alpha[q, at, :])
            weights[q, at, :] = hi
            weights[KSEG + q, at, :] = mid
        colour = jnp.concatenate([coef[q, 6:9, :]] * 3 + [jnp.zeros((LANES - 9, span), F32)], 0).T
        c_hi, c_mid = split2(colour)
        shown = shown + dot(weights[q], c_hi) + dot(weights[q], c_mid) + dot(weights[KSEG + q], c_hi)
    shot = shown.T
    image[0] = shot[0:3, :]
    goal = jnp.concatenate([target[0]] * 3 + [jnp.zeros((LANES - 9, pixels), F32)], 0)
    err_rows = (shot - goal)[:ROWS]
    err = shown - goal.T
    e_hi, e_mid = split2(err)
    e_cols = jnp.where(lane < 6, e_hi.astype(F32), e_mid.astype(F32)).astype(BF16)
    er_hi, er_mid = split2(err_rows)
    behind = jnp.zeros((pixels, 1), F32)
    for q in range(KSEG):
        col = coef[q, 6:9, :]
        hi, mid = split2(col)
        hi, mid = hi.astype(F32), mid.astype(F32)
        c_rows = jnp.concatenate([hi, mid, hi, jnp.zeros((LANES - 9, span), F32)], 0).astype(BF16)
        gback2 = dot(e_cols, c_rows)
        w_hi, w_mid = weights[q], weights[KSEG + q]
        dcol = dot(er_hi, w_hi) + dot(er_hi, w_mid) + dot(er_mid, w_hi)
        dpar[q, 6:9, :] = dcol[0:3]
        for y in range(SIDE):
            at = slice(y * SIDE, (y + 1) * SIDE)
            gt = gback2[at] * trans[q, at, :]
            trans[q, at, :] = gt
            hi, mid = split2(gt * alpha[q, at, :])
            logs[q, at, :span] = hi
            logs[q, at, span:] = mid
        backs[q] = dot(logs[q], lower[1])
    for q in reversed(range(KSEG)):
        gback[...] = jnp.broadcast_to(behind, (pixels, LANES))
        behind = behind + backs[q, :, 0:1] + trans[q, :, 0:1] * alpha[q, :, 0:1]
        sa, sc, cross, ex, ey, th = par[q]
        dx = dxs[q]
        d0 = jnp.zeros((SIDE, span), F32)
        d1 = jnp.zeros((SIDE, span), F32)
        d2 = jnp.zeros((SIDE, span), F32)
        for y in range(SIDE):
            at = slice(y * SIDE, (y + 1) * SIDE)
            both = jnp.concatenate([gback[at, :]] * halves, 1)
            al = alpha[q, at, :]
            d = (trans[q, at, :] - (backs[q, at, :] + both) / (1.0 - al)) * al
            ddy = d * dys[q, 0, y : y + 1, :]
            d0 = d0 + d
            d1 = d1 + ddy
            d2 = d2 + ddy * dys[q, 0, y : y + 1, :]
        m0 = jnp.sum(d0, 0, keepdims=True)
        m_x = jnp.sum(d0 * dx, 0, keepdims=True)
        m_y = jnp.sum(d1, 0, keepdims=True)
        m_xx = jnp.sum(d0 * dx * dx, 0, keepdims=True)
        m_xy = jnp.sum(d1 * dx, 0, keepdims=True)
        m_yy = jnp.sum(d2, 0, keepdims=True)
        dpar[q, 0:1, :] = sa * m_x + cross * m_y
        dpar[q, 1:2, :] = cross * m_x + sc * m_y
        dpar[q, 2:3, :] = -(sa * m_xx + cross * m_xy)
        dpar[q, 3:4, :] = -(sc * m_yy + cross * m_xy)
        dpar[q, 4:5, :] = -0.8 * (1.0 - th) * (1.0 + th) * ex * ey * m_xy
        dpar[q, 5:6, :] = m0 / (1.0 + jnp.exp(coef[q, 5:6, :]))
        dpar[q, nparam:, :] = jnp.zeros((ROWS - nparam, span), F32)
        parts = jnp.concatenate(split3(dpar[q]), 0)
        back = dot(parts, hots[q], ((1,), (1,)))
        back = back[:ROWS] + back[ROWS : 2 * ROWS] + back[2 * ROWS :]
        bufs[q * GROUP : q * GROUP + ROWS, :] = back
        bufs[q * GROUP + ROWS : (q + 1) * GROUP, :] = jnp.zeros((GROUP - ROWS, slots), F32)
    grads[...] = bufs[...].T.reshape(ndev, cap, LANES)


def update_kernel(
    segs, cap, perm, returned, ids_in, params, moment, second, new_params, new_moment, new_second, gathered
):
    ndev, rows, _ = ids_in.shape
    nparam, owned = params.shape
    group = iota((cap, LANES), 1) // GROUP

    def collect(r, carry):
        block = jnp.zeros((cap, LANES), F32)
        for s in range(segs):
            v = perm[r * segs + s]
            block = block + jnp.where(group == v % KSEG, returned[v // KSEG], 0.0)
        gathered[pl.ds(r, cap, stride=ndev), :] = block
        return carry

    lax.fori_loop(0, ndev, collect, 0, unroll=4)
    hot = one_hot_rows(ids_in[:, rows - 1, :], cap, owned)
    flat = gathered[...].T
    values = sum(flat[q * GROUP : q * GROUP + ROWS] for q in range(KSEG))
    parts = jnp.concatenate(split3(values), 0)
    grad = dot(parts, hot)
    grad = (grad[:ROWS] + grad[ROWS : 2 * ROWS] + grad[2 * ROWS :])[:nparam]
    m = 0.9 * moment[...] + 0.1 * grad
    v = 0.99 * second[...] + 0.01 * grad * grad
    new_moment[...] = m
    new_second[...] = v
    new_params[...] = params[...] - 0.05 * m / (jnp.sqrt(v) + 1e-08)


def per_device(params, moment, second, fetch_ids, seg_ids, seg_count, seg_perm, target):
    ndev = lax.axis_size("dev")
    nparam, owned = params.shape
    segs, span = seg_ids.shape
    cap = fetch_ids.shape[2]
    pixels = target.shape[2]
    slots = ndev * cap
    rows = segs * span // LANES
    assert target.shape[0] == 1 and segs == KSEG and rows == cap and pixels == SIDE * SIDE
    fetch = jnp.pad(fetch_ids[0], ((0, 0), (0, LANES - cap)))
    block = jax.ShapeDtypeStruct((ndev, rows, LANES), F32)
    swap = functools.partial(lax.all_to_all, axis_name="dev", split_axis=0, concat_axis=0, tiled=True)

    requests, moved = pl.pallas_call(
        functools.partial(request_kernel, cap),
        out_shape=(jax.ShapeDtypeStruct((ndev, rows, LANES), jnp.int32), jax.ShapeDtypeStruct((rows, LANES), F32)),
        in_specs=[SMEM, VMEM, VMEM],
        out_specs=(VMEM, VMEM),
        scratch_shapes=[pltpu.VMEM((rows, LANES), jnp.int32)],
        compiler_params=PARAMS,
        name="requests",
    )(seg_count, seg_ids, fetch)
    lists = swap(requests)
    outgoing, order = pl.pallas_call(
        functools.partial(send_kernel, segs, cap),
        out_shape=(block, jax.ShapeDtypeStruct(seg_perm.shape, jnp.int32)),
        in_specs=[SMEM, VMEM, VMEM, VMEM],
        out_specs=(VMEM, SMEM),
        scratch_shapes=[pltpu.VMEM((LANES, owned), F32), pltpu.VMEM((slots, LANES), F32)],
        compiler_params=PARAMS,
        name="send",
    )(seg_perm, lists, params, moved)
    arrived = swap(outgoing)
    me = lax.axis_index("dev").astype(jnp.int32).reshape(1)
    image, grads = pl.pallas_call(
        functools.partial(render_kernel, segs, cap, nparam),
        out_shape=(jax.ShapeDtypeStruct(target.shape, F32), block),
        in_specs=[SMEM, SMEM, VMEM, VMEM, VMEM],
        out_specs=(VMEM, VMEM),
        scratch_shapes=[
            pltpu.VMEM((LANES, slots), F32),
            pltpu.VMEM((KSEG, slots, span), BF16),
            pltpu.VMEM((KSEG, ROWS, span), F32),
            pltpu.VMEM((KSEG, span), jnp.int32),
            pltpu.VMEM((KSEG, pixels, span), F32),
            pltpu.VMEM((KSEG, pixels, span), F32),
            pltpu.VMEM((KSEG, pixels, 2 * span), BF16),
            pltpu.VMEM((2 * KSEG, pixels, span), BF16),
            pltpu.VMEM((KSEG, pixels, span), F32),
            pltpu.VMEM((2, 2 * span, span), BF16),
            pltpu.VMEM((KSEG, 2, SIDE, span), F32),
            pltpu.VMEM((KSEG, ROWS, span), F32),
            pltpu.VMEM((pixels, LANES), F32),
        ],
        compiler_params=PARAMS,
        name="render",
    )(me, order, arrived, lists, target)
    returned = swap(grads)
    new = jax.ShapeDtypeStruct(params.shape, F32)
    new_params, new_moment, new_second = pl.pallas_call(
        functools.partial(update_kernel, segs, cap),
        out_shape=(new, new, new),
        in_specs=[SMEM] + [VMEM] * 5,
        out_specs=(VMEM, VMEM, VMEM),
        scratch_shapes=[pltpu.VMEM((slots, LANES), F32)],
        compiler_params=PARAMS,
        name="update",
    )(seg_perm, returned, lists, params, moment, second)
    return (image, new_params, new_moment, new_second)


def solution(mesh):
    placed = (
        P(None, "dev"),
        P(None, "dev"),
        P(None, "dev"),
        P("dev", None, None),
        P("dev", None),
        P("dev"),
        P(),
        P("dev", None, None),
    )
    return jax.shard_map(
        per_device,
        mesh=mesh,
        in_specs=placed,
        out_specs=(P("dev", None, None), P(None, "dev"), P(None, "dev"), P(None, "dev")),
        check_vma=False,
    )
```

```python
import functools

import jax
import jax.numpy as jnp
from jax import lax
from jax.experimental import pallas as pl
from jax.experimental.pallas import tpu as pltpu
from jax.sharding import PartitionSpec as P

TILES_X = 8
KSEG = 4
SIDE = 16
LANES = 128
SUB = 8
ROWS = 16
F32 = jnp.float32
BF16 = jnp.bfloat16
SMEM = pl.BlockSpec(memory_space=pltpu.SMEM)
VMEM = pl.BlockSpec(memory_space=pltpu.VMEM)
HBM = pl.BlockSpec(memory_space=pltpu.HBM)
PARAMS = pltpu.CompilerParams(vmem_limit_bytes=40 * 2**20)


def split2(x):
    high = x.astype(BF16)
    return high, (x - high.astype(F32)).astype(BF16)


def split3(x):
    high = x.astype(BF16)
    rest = x - high.astype(F32)
    mid = rest.astype(BF16)
    return high, mid, (rest - mid.astype(F32)).astype(BF16)


def iota(shape, dim):
    return lax.broadcasted_iota(jnp.int32, shape, dim)


def dot(a, b, dims=((1,), (0,))):
    return lax.dot_general(a, b, (dims, ((), ())), preferred_element_type=F32)


def stages(ndev):
    top, place, out = ndev.bit_length() - 1, 0, []
    assert ndev == 1 << top and top >= 3
    while top > 1:
        bits = min(2, top - 1)
        top -= bits
        out.append((top, bits, place))
        place += bits
    return out + [(0, 1, place)]


def position(ndev, offset):
    return sum(((offset >> bit) & ((1 << bits) - 1)) << place for bit, bits, place in stages(ndev))


def offset_at(ndev, pos):
    return sum(((pos >> place) & ((1 << bits) - 1)) << bit for bit, bits, place in stages(ndev))


def gather_blocks(block, ndev, beside):
    def pull(x, change):
        return lax.ppermute(x, "dev", [(d, d ^ change) for d in range(ndev)])

    held, steps = [block[None]], stages(ndev)
    for number, (bit, bits, _) in enumerate(steps[:-1]):
        whole = held[0] if len(held) == 1 else jnp.concatenate(held, 0)
        if number == 1:
            whole, beside = lax.optimization_barrier((whole, beside))
        held = [whole] + [pull(whole, change << bit) for change in range(1, 1 << bits)]
    return held + [pull(x, 1) for x in held], beside


def pick(source, lanes):
    return jnp.take_along_axis(source, lanes, axis=1)


def pack_kernel(count_in, seg_in, fetch_in, params_in, out, count, seg, fetch, params, sems):
    segs, span = seg.shape
    nparam, owned = params.shape
    chunks, halves = owned // LANES, span // LANES
    lane = iota((1, LANES), 1)
    pairs = ((params_in, params), (seg_in, seg), (fetch_in, fetch), (count_in, count))
    copies = [pltpu.make_async_copy(a, b, sems.at[i]) for i, (a, b) in enumerate(pairs)]
    for copy in copies:
        copy.start()
    for copy in copies:
        copy.wait()
    for p in range(nparam):
        for c in range(chunks):
            out[p * chunks + c : p * chunks + c + 1, :] = params[p : p + 1, c * LANES : (c + 1) * LANES]
    at = nparam * chunks
    for s in range(segs):
        for h in range(halves):
            row = jnp.where(lane + h * LANES < count[s], seg[s : s + 1, h * LANES : (h + 1) * LANES], -1)
            out[at : at + 1, :] = row.astype(F32)
            at += 1
    out[at : at + SUB, :] = jnp.zeros((SUB, LANES), F32)
    out[at : at + SUB, : fetch.shape[1]] = fetch[...].astype(F32)


def layout_kernel(perm, target, order, tri, goal, goal_cols):
    def place(j, carry):
        order[perm[j]] = j
        return carry

    lax.fori_loop(0, perm.shape[0], place, 0, unroll=8)
    span = tri.shape[2]
    src, dst = iota((span, span), 0), iota((span, span), 1)
    before = (src < dst).astype(F32).astype(BF16)
    after = (src > dst).astype(F32).astype(BF16)
    for half in range(2):
        tri[0, half * span : (half + 1) * span, :] = before
        tri[1, half * span : (half + 1) * span, :] = after
    rows = target[0]
    pixels = rows.shape[1]
    wide = jnp.concatenate([rows] * 3 + [jnp.zeros((LANES - 9, pixels), F32)], 0)
    goal[...] = wide[:ROWS]
    goal_cols[...] = wide.T


def render_kernel(segs, cap, nparam, chunks, ndev, *refs):
    me_ref, order, tri, goal, goal_cols = refs[:5]
    narr = 2 << stages(ndev)[-2][1]
    arrays = refs[5 : 5 + narr]
    image, grads = refs[5 + narr : 7 + narr]
    (idrows, table, hots, coef, alpha, trans, logs, weights, backs, dys, dpar, gback, flat) = refs[7 + narr :]
    per = arrays[0].shape[0]
    slots = ndev * cap
    quarter = slots // 2
    pixels = SIDE * SIDE
    span = hots.shape[2]
    halves = span // LANES
    me = me_ref[0]
    base = nparam * chunks

    def block(j):
        return arrays[j // per], j % per

    for j in range(ndev):
        ref, at = block(j)
        idrows[j] = ref[at, base : base + 2 * SUB, :]
    fetched, listed = [], []
    for q in range(KSEG):
        slot = order[me * KSEG + q]
        j = position(ndev, (slot // segs) ^ me)
        fetched.append(idrows[j, SUB : 2 * SUB, :])
        s = slot % segs
        listed.append([idrows[j, pl.ds(s * halves + h, 1), :].astype(jnp.int32) for h in range(halves)])
    sub, lane = iota((SUB, LANES), 0), iota((SUB, LANES), 1)
    rank, which = (lane // cap) % KSEG, lane // (cap * KSEG)
    for g in range(ndev // 4):
        offs = [offset_at(ndev, 4 * g + b) for b in range(4)]
        off = jnp.where(which == 0, offs[0], jnp.where(which == 1, offs[1], jnp.where(which == 2, offs[2], offs[3])))
        owner = off ^ me
        found = jnp.zeros((SUB, LANES), F32)
        for q in range(KSEG):
            found = jnp.where(rank == q, pick(fetched[q], owner), found)
        local = jnp.sum(jnp.where(sub == lane % cap, found, 0.0), 0, keepdims=True).astype(jnp.int32)
        local = jnp.broadcast_to(local, (SUB, LANES))
        inside, chunk = local % LANES, local // LANES
        for p in range(nparam):
            got = jnp.zeros((SUB, LANES), F32)
            for b in range(4):
                ref, at = block(4 * g + b)
                got = jnp.where(which == b, pick(ref[at, p * chunks : (p + 1) * chunks, :], inside), got)
            table[g, p : p + 1, :] = jnp.sum(jnp.where(sub == chunk, got, 0.0), 0, keepdims=True)
    slot_row = iota((slots, span), 0)
    fine = (iota((SIDE, span), 0).astype(F32) + 0.5) / SIDE
    pos_x = (me % TILES_X).astype(F32) + fine
    pos_y = (me // TILES_X).astype(F32) + fine

    par, dxs = [], []
    for q in range(KSEG):
        for h in range(halves):
            row = listed[q][h]
            live = row >= 0
            row = jnp.maximum(row, 0)
            pos = position(ndev, (row // cap) ^ me)
            spot = jnp.broadcast_to((pos % 4) * (cap * KSEG) + q * cap + row % cap, (SUB, LANES))
            team = pos // 4
            low = jnp.zeros((SUB, LANES), F32)
            high = jnp.zeros((SUB, LANES), F32)
            for g in range(ndev // 4):
                low = jnp.where(team == g, pick(table[g, :SUB, :], spot), low)
                high = jnp.where(team == g, pick(table[g, SUB:, :], spot), high)
            cols = slice(h * LANES, (h + 1) * LANES)
            coef[q, :SUB, cols] = jnp.where(live, low, 0.0)
            coef[q, SUB:, cols] = jnp.where(live, high, 0.0)
        own = jnp.concatenate(listed[q], 1)
        live = (own >= 0).astype(F32)
        k = own % cap
        own = jnp.where(own >= 0, (k // 4) * quarter + (own // cap) * 4 + k % 4, -1)
        hots[q] = (slot_row == own).astype(F32).astype(BF16)
        got = coef[q]
        mx, my = got[0:1], got[1:2]
        ex, ey = jnp.exp(got[2:3]), jnp.exp(got[3:4])
        th = jnp.tanh(got[4:5])
        sa, sc, cross = ex * ex, ey * ey, 0.8 * th * ex * ey
        peak = 0.95 / (1.0 + jnp.exp(-got[5:6])) * live
        dx = pos_x - mx
        dy = pos_y - my
        xa = -0.5 * sa * dx * dx
        xb = -cross * dx
        dys[q, 0] = dy
        dys[q, 1] = -0.5 * sc * dy * dy
        par.append((sa, sc, cross, ex, ey, th))
        dxs.append(dx)
        for y in range(SIDE):
            power = xa + dys[q, 0, y : y + 1, :] * xb + dys[q, 1, y : y + 1, :]
            al = peak * jnp.exp(power)
            at = slice(y * SIDE, (y + 1) * SIDE)
            alpha[q, at, :] = al
            hi, mid = split2(jnp.log(1.0 - al))
            logs[q, at, :span] = hi
            logs[q, at, span:] = mid
        trans[q] = dot(logs[q], tri[0])

    ahead = jnp.zeros((pixels, 1), F32)
    shown = jnp.zeros((pixels, LANES), F32)
    lane = iota((pixels, LANES), 1)
    for q in range(KSEG):
        gback[...] = jnp.broadcast_to(ahead, (pixels, LANES))
        ahead = ahead + trans[q, :, span - 1 : span] + jnp.log(1.0 - alpha[q, :, span - 1 : span])
        for y in range(SIDE):
            at = slice(y * SIDE, (y + 1) * SIDE)
            both = jnp.concatenate([gback[at, :]] * halves, 1)
            t = jnp.exp(trans[q, at, :] + both)
            trans[q, at, :] = t
            hi, mid = split2(t * alpha[q, at, :])
            weights[q, at, :] = hi
            weights[KSEG + q, at, :] = mid
        colour = jnp.concatenate([coef[q, 6:9, :]] * 3 + [jnp.zeros((LANES - 9, span), F32)], 0).T
        c_hi, c_mid = split2(colour)
        shown = shown + dot(weights[q], c_hi) + dot(weights[q], c_mid) + dot(weights[KSEG + q], c_hi)
    shot = shown.T
    image[0] = shot[0:3, :]
    err = shown - goal_cols[...]
    e_hi, e_mid = split2(err)
    e_cols = jnp.where(lane < 6, e_hi.astype(F32), e_mid.astype(F32)).astype(BF16)
    er_hi, er_mid = split2(shot[:ROWS] - goal[...])
    behind = jnp.zeros((pixels, 1), F32)
    for q in range(KSEG):
        hi, mid = split2(coef[q, 6:9, :])
        hi, mid = hi.astype(F32), mid.astype(F32)
        c_rows = jnp.concatenate([hi, mid, hi, jnp.zeros((LANES - 9, span), F32)], 0).astype(BF16)
        slope = dot(e_cols, c_rows)
        w_hi, w_mid = weights[q], weights[KSEG + q]
        dcol = dot(er_hi, w_hi) + dot(er_hi, w_mid) + dot(er_mid, w_hi)
        dpar[q, 6:9, :] = dcol[0:3]
        for y in range(SIDE):
            at = slice(y * SIDE, (y + 1) * SIDE)
            gt = slope[at] * trans[q, at, :]
            trans[q, at, :] = gt
            hi, mid = split2(gt * alpha[q, at, :])
            logs[q, at, :span] = hi
            logs[q, at, span:] = mid
        backs[q] = dot(logs[q], tri[1])
    for q in reversed(range(KSEG)):
        gback[...] = jnp.broadcast_to(behind, (pixels, LANES))
        behind = behind + backs[q, :, 0:1] + trans[q, :, 0:1] * alpha[q, :, 0:1]
        sa, sc, cross, ex, ey, th = par[q]
        dx = dxs[q]
        d0 = jnp.zeros((SIDE, span), F32)
        d1 = jnp.zeros((SIDE, span), F32)
        d2 = jnp.zeros((SIDE, span), F32)
        for y in range(SIDE):
            at = slice(y * SIDE, (y + 1) * SIDE)
            both = jnp.concatenate([gback[at, :]] * halves, 1)
            al = alpha[q, at, :]
            d = (trans[q, at, :] - (backs[q, at, :] + both) / (1.0 - al)) * al
            ddy = d * dys[q, 0, y : y + 1, :]
            d0 = d0 + d
            d1 = d1 + ddy
            d2 = d2 + ddy * dys[q, 0, y : y + 1, :]
        m0 = jnp.sum(d0, 0, keepdims=True)
        m_x = jnp.sum(d0 * dx, 0, keepdims=True)
        m_y = jnp.sum(d1, 0, keepdims=True)
        m_xx = jnp.sum(d0 * dx * dx, 0, keepdims=True)
        m_xy = jnp.sum(d1 * dx, 0, keepdims=True)
        m_yy = jnp.sum(d2, 0, keepdims=True)
        dpar[q, 0:1, :] = sa * m_x + cross * m_y
        dpar[q, 1:2, :] = cross * m_x + sc * m_y
        dpar[q, 2:3, :] = -(sa * m_xx + cross * m_xy)
        dpar[q, 3:4, :] = -(sc * m_yy + cross * m_xy)
        dpar[q, 4:5, :] = -0.8 * (1.0 - th) * (1.0 + th) * ex * ey * m_xy
        dpar[q, 5:6, :] = m0 / (1.0 + jnp.exp(coef[q, 5:6, :]))
        dpar[q, nparam:, :] = jnp.zeros((ROWS - nparam, span), F32)
        parts = jnp.concatenate(split3(dpar[q]), 0)
        back = dot(parts, hots[q], ((1,), (1,)))
        back = back[:ROWS] + back[ROWS : 2 * ROWS] + back[2 * ROWS :]
        for half in range(2):
            row = half * KSEG * ROWS + q * ROWS
            flat[row : row + ROWS, :] = back[:, half * quarter : (half + 1) * quarter]
    turned = flat[...].T
    for o in range(ndev):
        grads[o] = turned[4 * o : 4 * o + 4, :]


def asked_kernel(cap, base, ndev, owned, me_ref, *refs):
    *arrays, hot, column = refs
    per = arrays[0].shape[0]
    rows = ndev * 4
    for j in range(ndev):
        wide = arrays[j // per][j % per, base : base + cap, :]
        column[4 * j : 4 * j + 4, :] = wide[:4]
        column[rows + 4 * j : rows + 4 * j + 4, :] = wide[4:]
    mine = iota(column.shape, 1) == me_ref[0]
    ids = jnp.sum(jnp.where(mine, column[...], 0.0), 1, keepdims=True).astype(jnp.int32)
    for c in range(owned // LANES):
        cols = iota(column.shape, 1) + c * LANES
        hot[:, c * LANES : (c + 1) * LANES] = (ids == cols).astype(F32).astype(BF16)


def update_kernel(segs, ndev, me_ref, perm, returned, hot, params, moment, second, new_params, new_moment, new_second, held):
    nparam = params.shape[0]
    rank = (iota((4, LANES), 1) // ROWS) % KSEG
    me = me_ref[0]
    for j in range(ndev):
        r = offset_at(ndev, j) ^ me
        block = jnp.zeros((4, LANES), F32)
        for s in range(segs):
            v = perm[r * segs + s]
            block = block + jnp.where(rank == v % KSEG, returned[v // KSEG], 0.0)
        held[4 * j : 4 * j + 4, :] = block
    flat = held[...].T
    half = KSEG * ROWS
    sides = [sum(flat[h * half + q * ROWS : h * half + (q + 1) * ROWS] for q in range(KSEG)) for h in range(2)]
    parts = jnp.concatenate(split3(jnp.concatenate(sides, 1)), 0)
    grad = dot(parts, hot[...])
    grad = (grad[:ROWS] + grad[ROWS : 2 * ROWS] + grad[2 * ROWS :])[:nparam]
    m = 0.9 * moment[...] + 0.1 * grad
    v = 0.99 * second[...] + 0.01 * grad * grad
    new_moment[...] = m
    new_second[...] = v
    new_params[...] = params[...] - 0.05 * m / (jnp.sqrt(v) + 1e-08)


def per_device(params, moment, second, fetch_ids, seg_ids, seg_count, seg_perm, target):
    ndev = lax.axis_size("dev")
    nparam, owned = params.shape
    segs, span = seg_ids.shape
    cap = fetch_ids.shape[2]
    pixels = target.shape[2]
    slots = ndev * cap
    chunks = owned // LANES
    lists = segs * span // LANES
    assert target.shape[0] == 1 and segs == KSEG and pixels == SIDE * SIDE
    assert cap == SUB and chunks == SUB and lists == SUB and ndev <= LANES
    base = nparam * chunks
    me = lax.axis_index("dev").astype(jnp.int32).reshape(1)

    in_hbm = functools.partial(pltpu.with_memory_space_constraint, memory_space=pltpu.HBM)

    packed = pl.pallas_call(
        pack_kernel,
        out_shape=jax.ShapeDtypeStruct((base + 2 * SUB, LANES), F32),
        in_specs=[HBM] * 4,
        out_specs=VMEM,
        scratch_shapes=[
            pltpu.SMEM(seg_count.shape, jnp.int32),
            pltpu.VMEM(seg_ids.shape, jnp.int32),
            pltpu.VMEM((cap, ndev), jnp.int32),
            pltpu.VMEM(params.shape, F32),
            pltpu.SemaphoreType.DMA((4,)),
        ],
        compiler_params=PARAMS,
        name="pack",
    )(*[in_hbm(x) for x in (seg_count, seg_ids, fetch_ids[0].T, params)])
    order, tri, goal, goal_cols = pl.pallas_call(
        layout_kernel,
        out_shape=(
            jax.ShapeDtypeStruct(seg_perm.shape, jnp.int32),
            jax.ShapeDtypeStruct((2, 2 * span, span), BF16),
            jax.ShapeDtypeStruct((ROWS, pixels), F32),
            jax.ShapeDtypeStruct((pixels, LANES), F32),
        ),
        in_specs=[SMEM, VMEM],
        out_specs=(SMEM, VMEM, VMEM, VMEM),
        compiler_params=PARAMS,
        cost_estimate=pl.CostEstimate(flops=0, bytes_accessed=4 * 2**20, transcendentals=0),
        name="layout",
    )(seg_perm, target)
    blocks, (order, tri, goal, goal_cols) = gather_blocks(packed, ndev, (order, tri, goal, goal_cols))
    image, grads = pl.pallas_call(
        functools.partial(render_kernel, segs, cap, nparam, chunks, ndev),
        out_shape=(jax.ShapeDtypeStruct(target.shape, F32), jax.ShapeDtypeStruct((ndev, 4, LANES), F32)),
        in_specs=[SMEM, SMEM] + [VMEM] * (3 + len(blocks)),
        out_specs=(VMEM, VMEM),
        scratch_shapes=[
            pltpu.VMEM((ndev, 2 * SUB, LANES), F32),
            pltpu.VMEM((ndev // 4, ROWS, LANES), F32),
            pltpu.VMEM((KSEG, slots, span), BF16),
            pltpu.VMEM((KSEG, ROWS, span), F32),
            pltpu.VMEM((KSEG, pixels, span), F32),
            pltpu.VMEM((KSEG, pixels, span), F32),
            pltpu.VMEM((KSEG, pixels, 2 * span), BF16),
            pltpu.VMEM((2 * KSEG, pixels, span), BF16),
            pltpu.VMEM((KSEG, pixels, span), F32),
            pltpu.VMEM((KSEG, 2, SIDE, span), F32),
            pltpu.VMEM((KSEG, ROWS, span), F32),
            pltpu.VMEM((pixels, LANES), F32),
            pltpu.VMEM((LANES, slots // 2), F32),
        ],
        compiler_params=PARAMS,
        name="render",
    )(me, order, tri, goal, goal_cols, *blocks)
    returned = lax.all_to_all(grads, "dev", split_axis=0, concat_axis=0, tiled=True)
    hot = pl.pallas_call(
        functools.partial(asked_kernel, cap, base + SUB, ndev, owned),
        out_shape=jax.ShapeDtypeStruct((slots, owned), BF16),
        in_specs=[SMEM] + [VMEM] * len(blocks),
        out_specs=VMEM,
        scratch_shapes=[pltpu.VMEM((slots, LANES), F32)],
        compiler_params=PARAMS,
        name="asked",
    )(me, *blocks)
    new = jax.ShapeDtypeStruct(params.shape, F32)
    new_params, new_moment, new_second = pl.pallas_call(
        functools.partial(update_kernel, segs, ndev),
        out_shape=(new, new, new),
        in_specs=[SMEM, SMEM] + [VMEM] * 5,
        out_specs=(VMEM, VMEM, VMEM),
        scratch_shapes=[pltpu.VMEM((slots // 2, LANES), F32)],
        compiler_params=PARAMS,
        name="update",
    )(me, seg_perm, returned, hot, params, moment, second)
    return (image, new_params, new_moment, new_second)


def solution(mesh):
    placed = (
        P(None, "dev"),
        P(None, "dev"),
        P(None, "dev"),
        P("dev", None, None),
        P("dev", None),
        P("dev"),
        P(),
        P("dev", None, None),
    )
    return jax.shard_map(
        per_device,
        mesh=mesh,
        in_specs=placed,
        out_specs=(P("dev", None, None), P(None, "dev"), P(None, "dev"), P(None, "dev")),
        check_vma=False,
    )
```

```python
import functools

import jax
import jax.numpy as jnp
from jax import lax
from jax.experimental import pallas as pl
from jax.experimental.pallas import tpu as pltpu
from jax.sharding import PartitionSpec as P

TILES_X = 8
KSEG = 4
SIDE = 16
LANES = 128
SUB = 8
ROWS = 16
F32 = jnp.float32
BF16 = jnp.bfloat16
SMEM = pl.BlockSpec(memory_space=pltpu.SMEM)
VMEM = pl.BlockSpec(memory_space=pltpu.VMEM)
HBM = pl.BlockSpec(memory_space=pltpu.HBM)
PARAMS = pltpu.CompilerParams(vmem_limit_bytes=40 * 2**20)


def split2(x):
    high = x.astype(BF16)
    return high, (x - high.astype(F32)).astype(BF16)


def split3(x):
    high = x.astype(BF16)
    rest = x - high.astype(F32)
    mid = rest.astype(BF16)
    return high, mid, (rest - mid.astype(F32)).astype(BF16)


def iota(shape, dim):
    return lax.broadcasted_iota(jnp.int32, shape, dim)


def dot(a, b, dims=((1,), (0,))):
    return lax.dot_general(a, b, (dims, ((), ())), preferred_element_type=F32)


def stages(ndev):
    top, place, out = ndev.bit_length() - 1, 0, []
    assert ndev == 1 << top and top >= 3
    while top > 1:
        bits = min(2, top - 1)
        top -= bits
        out.append((top, bits, place))
        place += bits
    return out + [(0, 1, place)]


def position(ndev, offset):
    return sum(((offset >> bit) & ((1 << bits) - 1)) << place for bit, bits, place in stages(ndev))


def offset_at(ndev, pos):
    return sum(((pos >> place) & ((1 << bits) - 1)) << bit for bit, bits, place in stages(ndev))


def gather_blocks(block, ndev, beside):
    def pull(x, change):
        return lax.ppermute(x, "dev", [(d, d ^ change) for d in range(ndev)])

    held, steps = [block[None]], stages(ndev)
    for number, (bit, bits, _) in enumerate(steps[:-1]):
        whole = held[0] if len(held) == 1 else jnp.concatenate(held, 0)
        if number == 1:
            whole, beside = lax.optimization_barrier((whole, beside))
        held = [whole] + [pull(whole, change << bit) for change in range(1, 1 << bits)]
    return held + [pull(x, 1) for x in held], beside


def pick(source, lanes):
    return jnp.take_along_axis(source, lanes, axis=1)


def sum_rows(blocks):
    row = iota((SUB, LANES), 0)
    for step in (1, 2, 4):
        first = row & step == 0
        blocks = [
            jnp.where(first, a, b) + pltpu.roll(jnp.where(first, b, a), step, 0)
            for a, b in zip(blocks[::2], blocks[1::2], strict=True)
        ]
    return blocks[0]


def pack_kernel(count_in, seg_in, fetch_in, params_in, out, count, seg, fetch, params, sems):
    segs, span = seg.shape
    nparam, owned = params.shape
    chunks, halves = owned // LANES, span // LANES
    lane = iota((1, LANES), 1)
    pairs = ((params_in, params), (seg_in, seg), (fetch_in, fetch), (count_in, count))
    copies = [pltpu.make_async_copy(a, b, sems.at[i]) for i, (a, b) in enumerate(pairs)]
    for copy in copies:
        copy.start()
    for copy in copies:
        copy.wait()
    for p in range(nparam):
        for c in range(chunks):
            out[p * chunks + c : p * chunks + c + 1, :] = params[p : p + 1, c * LANES : (c + 1) * LANES]
    at = nparam * chunks
    for s in range(segs):
        for h in range(halves):
            row = jnp.where(lane + h * LANES < count[s], seg[s : s + 1, h * LANES : (h + 1) * LANES], -1)
            out[at : at + 1, :] = row.astype(F32)
            at += 1
    out[at : at + SUB, :] = jnp.zeros((SUB, LANES), F32)
    out[at : at + SUB, : fetch.shape[1]] = fetch[...].astype(F32)


def layout_kernel(perm, target, order, tri, goal, goal_cols):
    def place(j, carry):
        order[perm[j]] = j
        return carry

    lax.fori_loop(0, perm.shape[0], place, 0, unroll=8)
    span = tri.shape[2]
    src, dst = iota((span, span), 0), iota((span, span), 1)
    before = (src < dst).astype(F32).astype(BF16)
    after = (src > dst).astype(F32).astype(BF16)
    for half in range(2):
        tri[0, half * span : (half + 1) * span, :] = before
        tri[1, half * span : (half + 1) * span, :] = after
    rows = jnp.concatenate([target[c] for c in range(3)], 0)
    pixels = rows.shape[1]
    wide = jnp.concatenate([rows] * 3 + [jnp.zeros((LANES - 9, pixels), F32)], 0)
    goal[...] = wide[:ROWS]
    goal_cols[...] = wide.T


def render_kernel(segs, cap, nparam, chunks, ndev, *refs):
    me_ref, order, tri, goal, goal_cols = refs[:5]
    narr = 2 << stages(ndev)[-2][1]
    arrays = refs[5 : 5 + narr]
    image, grads = refs[5 + narr : 7 + narr]
    (ids, lists, idrows, table, hots, coef, alpha, trans, logs, weights, colours, backs, dys, dpar, gback, flat) = refs[7 + narr :]
    per = arrays[0].shape[0]
    slots = ndev * cap
    quarter = slots // 2
    pixels = SIDE * SIDE
    span = hots.shape[1]
    halves = span // LANES
    me = me_ref[0]
    base = nparam * chunks

    def block(j):
        return arrays[j // per], j % per

    for j in range(ndev):
        ref, at = block(j)
        idrows[j] = ref[at, base : base + 2 * SUB, :]
    fetched = []
    for q in range(KSEG):
        slot = order[me * KSEG + q]
        j = position(ndev, (slot // segs) ^ me)
        fetched.append(idrows[j, SUB : 2 * SUB, :])
        for h in range(halves):
            lists[q * halves + h : q * halves + h + 1, :] = idrows[j, pl.ds((slot % segs) * halves + h, 1), :]
    sub, lane = iota((SUB, LANES), 0), iota((SUB, LANES), 1)
    low_bits = cap.bit_length() - 1
    rank, which = (lane >> low_bits) & (KSEG - 1), lane >> (low_bits + 2)
    extra = []
    for g in range(ndev // 4):
        offs = [offset_at(ndev, 4 * g + b) for b in range(4)]
        off = jnp.where(which == 0, offs[0], jnp.where(which == 1, offs[1], jnp.where(which == 2, offs[2], offs[3])))
        owner = off ^ me
        found = jnp.zeros((SUB, LANES), F32)
        for q in range(KSEG):
            found = jnp.where(rank == q, pick(fetched[q], owner), found)
        found = jnp.where(sub == lane & (cap - 1), found, 0.0)
        for step in (4, 2, 1):
            found = found + pltpu.roll(found, step, 0)
        local = found.astype(jnp.int32)
        inside, chunk = local & (LANES - 1), local >> 7
        got = []
        for p in range(nparam):
            value = jnp.zeros((SUB, LANES), F32)
            for b in range(4):
                ref, at = block(4 * g + b)
                value = jnp.where(which == b, pick(ref[at, p * chunks : (p + 1) * chunks, :], inside), value)
            got.append(jnp.where(sub == chunk, value, 0.0))
        table[g] = sum_rows(got[:SUB])
        last = got[SUB]
        for step in (4, 2, 1):
            last = last + pltpu.roll(last, step, 0)
        extra.append(last)
    listed = lists[...].astype(jnp.int32)
    slot = jnp.maximum(listed, 0)
    pos = position(ndev, (slot >> low_bits) ^ me)
    spot = ((pos & 3) << (low_bits + 2)) + ((sub // halves) << low_bits) + (slot & (cap - 1))
    team = pos >> 2
    live = listed >= 0
    ninth = jnp.zeros((SUB, LANES), F32)
    for g in range(ndev // 4):
        ninth = jnp.where(team == g, pick(extra[g], spot), ninth)
    ninth = jnp.where(live, ninth, 0.0)
    k = slot & (cap - 1)
    into = jnp.where(live, (k >> 2) * quarter + (slot >> low_bits) * 4 + (k & 3), -1).astype(F32)
    for q in range(KSEG):
        for h in range(halves):
            row = q * halves + h
            cols = slice(h * LANES, (h + 1) * LANES)
            spot_row = jnp.broadcast_to(spot[row : row + 1, :], (SUB, LANES))
            team_row = jnp.broadcast_to(team[row : row + 1, :], (SUB, LANES))
            value = jnp.zeros((SUB, LANES), F32)
            for g in range(ndev // 4):
                value = jnp.where(team_row == g, pick(table[g], spot_row), value)
            coef[q, :SUB, cols] = jnp.where(live[row : row + 1, :], value, 0.0)
            coef[q, SUB : SUB + 1, cols] = ninth[row : row + 1, :]
            ids[q : q + 1, cols] = into[row : row + 1, :]
    thin = iota((span, LANES), 1)
    gap = jnp.zeros((ROWS - 9, span), F32)
    groups = []
    for q in range(KSEG):
        hi, mid = split2(coef[q, 6:9, :])
        groups += [hi.astype(F32)] * 3 + [gap] + [mid.astype(F32)] * 3 + [gap]
    columns = jnp.concatenate(groups, 0).T
    for q in range(KSEG):
        both = pltpu.roll(columns, LANES - 2 * q * ROWS, 1) if q else columns
        colours[2 * q * span : (2 * q + 1) * span, :] = jnp.where(thin < 2 * ROWS, both, 0.0).astype(BF16)
        colours[(2 * q + 1) * span : 2 * (q + 1) * span, :] = jnp.where(thin < ROWS, both, 0.0).astype(BF16)
    slot_lane = iota((span, slots), 1)
    fine = (iota((SIDE, span), 0).astype(F32) + 0.5) / SIDE
    pos_x = (me % TILES_X).astype(F32) + fine
    pos_y = (me // TILES_X).astype(F32) + fine

    par, dxs = [], []
    for q in range(KSEG):
        alive = (ids[q : q + 1, :] >= 0.0).astype(F32)
        got = coef[q]
        mx, my = got[0:1], got[1:2]
        ex, ey = jnp.exp(got[2:3]), jnp.exp(got[3:4])
        th = jnp.tanh(got[4:5])
        sa, sc, cross = ex * ex, ey * ey, 0.8 * th * ex * ey
        peak = 0.95 / (1.0 + jnp.exp(-got[5:6])) * alive
        dx = pos_x - mx
        dy = pos_y - my
        xa = -0.5 * sa * dx * dx
        xb = -cross * dx
        dys[q, 0] = dy
        dys[q, 1] = -0.5 * sc * dy * dy
        par.append((sa, sc, cross, ex, ey, th))
        dxs.append(dx)
        for y in range(SIDE):
            power = xa + dys[q, 0, y : y + 1, :] * xb + dys[q, 1, y : y + 1, :]
            al = peak * jnp.exp(power)
            at = slice(y * SIDE, (y + 1) * SIDE)
            alpha[q, at, :] = al
            hi, mid = split2(jnp.log(1.0 - al))
            logs[q, at, :span] = hi
            logs[q, at, span:] = mid
        trans[q] = dot(logs[q], tri[0])

    places = ids[...].T.astype(jnp.int32)
    for q in range(KSEG):
        hots[q] = (slot_lane == places[:, q : q + 1]).astype(F32).astype(BF16)
    ahead = jnp.zeros((pixels, 1), F32)
    lane = iota((pixels, LANES), 1)
    for q in range(KSEG):
        gback[...] = jnp.broadcast_to(ahead, (pixels, LANES))
        ahead = ahead + trans[q, :, span - 1 : span] + jnp.log(1.0 - alpha[q, :, span - 1 : span])
        for y in range(SIDE):
            at = slice(y * SIDE, (y + 1) * SIDE)
            both = jnp.concatenate([gback[at, :]] * halves, 1)
            t = jnp.exp(trans[q, at, :] + both)
            trans[q, at, :] = t
            hi, mid = split2(t * alpha[q, at, :])
            weights[at, 2 * q * span : (2 * q + 1) * span] = hi
            weights[at, (2 * q + 1) * span : 2 * (q + 1) * span] = mid
    shown = dot(weights[...], colours[...])
    e_hi, e_mid = split2(shown - goal_cols[...])
    e_cols = jnp.where((lane < 6) | (lane >= 9), e_hi.astype(F32), e_mid.astype(F32)).astype(BF16)
    shot = shown.T
    shot = shot[:ROWS] + shot[ROWS : 2 * ROWS]
    for c in range(3):
        image[c] = shot[c : c + 1, :]
    er_both = jnp.concatenate(split2(shot - goal[...]), 0)
    behind = jnp.zeros((pixels, 1), F32)
    for q in range(KSEG):
        hi, mid = split2(coef[q, 6:9, :])
        hi, mid = hi.astype(F32), mid.astype(F32)
        gap = jnp.zeros((ROWS - 9, span), F32)
        c_rows = jnp.concatenate([hi, mid, hi, gap, hi, jnp.zeros((LANES - ROWS - 3, span), F32)], 0).astype(BF16)
        slope = dot(e_cols, c_rows)
        dcol = dot(er_both, weights[:, 2 * q * span : (2 * q + 1) * span])
        dcol = dcol[:ROWS] + dcol[ROWS:] + dot(er_both[:ROWS], weights[:, (2 * q + 1) * span : 2 * (q + 1) * span])
        dpar[q, 6:9, :] = dcol[0:3]
        for y in range(SIDE):
            at = slice(y * SIDE, (y + 1) * SIDE)
            gt = slope[at] * trans[q, at, :]
            trans[q, at, :] = gt
            hi, mid = split2(gt * alpha[q, at, :])
            logs[q, at, :span] = hi
            logs[q, at, span:] = mid
        backs[q] = dot(logs[q], tri[1])
    for q in reversed(range(KSEG)):
        gback[...] = jnp.broadcast_to(behind, (pixels, LANES))
        behind = behind + backs[q, :, 0:1] + trans[q, :, 0:1] * alpha[q, :, 0:1]
        sa, sc, cross, ex, ey, th = par[q]
        dx = dxs[q]
        d0 = jnp.zeros((SIDE, span), F32)
        d1 = jnp.zeros((SIDE, span), F32)
        d2 = jnp.zeros((SIDE, span), F32)
        for y in range(SIDE):
            at = slice(y * SIDE, (y + 1) * SIDE)
            both = jnp.concatenate([gback[at, :]] * halves, 1)
            al = alpha[q, at, :]
            d = (trans[q, at, :] - (backs[q, at, :] + both) / (1.0 - al)) * al
            ddy = d * dys[q, 0, y : y + 1, :]
            d0 = d0 + d
            d1 = d1 + ddy
            d2 = d2 + ddy * dys[q, 0, y : y + 1, :]
        m0 = jnp.sum(d0, 0, keepdims=True)
        m_x = jnp.sum(d0 * dx, 0, keepdims=True)
        m_y = jnp.sum(d1, 0, keepdims=True)
        m_xx = jnp.sum(d0 * dx * dx, 0, keepdims=True)
        m_xy = jnp.sum(d1 * dx, 0, keepdims=True)
        m_yy = jnp.sum(d2, 0, keepdims=True)
        dpar[q, 0:1, :] = sa * m_x + cross * m_y
        dpar[q, 1:2, :] = cross * m_x + sc * m_y
        dpar[q, 2:3, :] = -(sa * m_xx + cross * m_xy)
        dpar[q, 3:4, :] = -(sc * m_yy + cross * m_xy)
        dpar[q, 4:5, :] = -0.8 * (1.0 - th) * (1.0 + th) * ex * ey * m_xy
        dpar[q, 5:6, :] = m0 / (1.0 + jnp.exp(coef[q, 5:6, :]))
        dpar[q, nparam:, :] = jnp.zeros((ROWS - nparam, span), F32)
        parts = jnp.concatenate(split3(dpar[q]), 0)
        back = dot(parts, hots[q])
        back = back[:ROWS] + back[ROWS : 2 * ROWS] + back[2 * ROWS :]
        for half in range(2):
            row = half * KSEG * ROWS + q * ROWS
            flat[row : row + ROWS, :] = back[:, half * quarter : (half + 1) * quarter]
    turned = flat[...].T
    for o in range(ndev):
        grads[o] = turned[4 * o : 4 * o + 4, :]


def asked_kernel(cap, base, ndev, owned, me_ref, *refs):
    *arrays, hot, column = refs
    per = arrays[0].shape[0]
    rows = ndev * 4
    for j in range(ndev):
        wide = arrays[j // per][j % per, base : base + cap, :]
        column[4 * j : 4 * j + 4, :] = wide[:4]
        column[rows + 4 * j : rows + 4 * j + 4, :] = wide[4:]
    mine = iota(column.shape, 1) == me_ref[0]
    ids = jnp.sum(jnp.where(mine, column[...], 0.0), 1, keepdims=True).astype(jnp.int32)
    for c in range(owned // LANES):
        cols = iota(column.shape, 1) + c * LANES
        hot[:, c * LANES : (c + 1) * LANES] = (ids == cols).astype(F32).astype(BF16)


def update_kernel(segs, ndev, me_ref, perm, returned, hot, params, moment, second, new_params, new_moment, new_second, held):
    nparam = params.shape[0]
    rank = (iota((4, LANES), 1) >> 4) & (KSEG - 1)
    me = me_ref[0]
    for j in range(ndev):
        r = offset_at(ndev, j) ^ me
        block = jnp.zeros((4, LANES), F32)
        for s in range(segs):
            v = perm[r * segs + s]
            block = block + jnp.where(rank == v & (KSEG - 1), returned[v >> 2], 0.0)
        held[4 * j : 4 * j + 4, :] = block
    flat = held[...].T
    half = KSEG * ROWS
    sides = [sum(flat[h * half + q * ROWS : h * half + (q + 1) * ROWS] for q in range(KSEG)) for h in range(2)]
    parts = jnp.concatenate(split3(jnp.concatenate(sides, 1)), 0)
    grad = dot(parts, hot[...])
    grad = (grad[:ROWS] + grad[ROWS : 2 * ROWS] + grad[2 * ROWS :])[:nparam]
    m = 0.9 * moment[...] + 0.1 * grad
    v = 0.99 * second[...] + 0.01 * grad * grad
    new_moment[...] = m
    new_second[...] = v
    new_params[...] = params[...] - 0.05 * m / (jnp.sqrt(v) + 1e-08)


def per_device(params, moment, second, fetch_ids, seg_ids, seg_count, seg_perm, target):
    ndev = lax.axis_size("dev")
    nparam, owned = params.shape
    segs, span = seg_ids.shape
    cap = fetch_ids.shape[2]
    pixels = target.shape[2]
    slots = ndev * cap
    chunks = owned // LANES
    lists = segs * span // LANES
    assert target.shape[0] == 1 and segs == KSEG and pixels == SIDE * SIDE
    assert cap == SUB and chunks == SUB and lists == SUB and ndev <= LANES and nparam == SUB + 1
    base = nparam * chunks
    me = lax.axis_index("dev").astype(jnp.int32).reshape(1)

    in_hbm = functools.partial(pltpu.with_memory_space_constraint, memory_space=pltpu.HBM)

    packed = pl.pallas_call(
        pack_kernel,
        out_shape=jax.ShapeDtypeStruct((base + 2 * SUB, LANES), F32),
        in_specs=[HBM] * 4,
        out_specs=VMEM,
        scratch_shapes=[
            pltpu.SMEM(seg_count.shape, jnp.int32),
            pltpu.VMEM(seg_ids.shape, jnp.int32),
            pltpu.VMEM((cap, ndev), jnp.int32),
            pltpu.VMEM(params.shape, F32),
            pltpu.SemaphoreType.DMA((4,)),
        ],
        compiler_params=PARAMS,
        name="pack",
    )(*[in_hbm(x) for x in (seg_count, seg_ids, fetch_ids[0].T, params)])
    order, tri, goal, goal_cols = pl.pallas_call(
        layout_kernel,
        out_shape=(
            jax.ShapeDtypeStruct(seg_perm.shape, jnp.int32),
            jax.ShapeDtypeStruct((2, 2 * span, span), BF16),
            jax.ShapeDtypeStruct((ROWS, pixels), F32),
            jax.ShapeDtypeStruct((pixels, LANES), F32),
        ),
        in_specs=[SMEM, VMEM],
        out_specs=(SMEM, VMEM, VMEM, VMEM),
        compiler_params=PARAMS,
        cost_estimate=pl.CostEstimate(flops=0, bytes_accessed=4 * 2**20, transcendentals=0),
        name="layout",
    )(seg_perm, target.transpose(1, 0, 2))
    blocks, (order, tri, goal, goal_cols) = gather_blocks(packed, ndev, (order, tri, goal, goal_cols))
    image, grads = pl.pallas_call(
        functools.partial(render_kernel, segs, cap, nparam, chunks, ndev),
        out_shape=(jax.ShapeDtypeStruct((3, 1, pixels), F32), jax.ShapeDtypeStruct((ndev, 4, LANES), F32)),
        in_specs=[SMEM, SMEM] + [VMEM] * (3 + len(blocks)),
        out_specs=(VMEM, VMEM),
        scratch_shapes=[
            pltpu.VMEM((SUB, span), F32),
            pltpu.VMEM((SUB, LANES), F32),
            pltpu.VMEM((ndev, 2 * SUB, LANES), F32),
            pltpu.VMEM((ndev // 4, SUB, LANES), F32),
            pltpu.VMEM((KSEG, span, slots), BF16),
            pltpu.VMEM((KSEG, ROWS, span), F32),
            pltpu.VMEM((KSEG, pixels, span), F32),
            pltpu.VMEM((KSEG, pixels, span), F32),
            pltpu.VMEM((KSEG, pixels, 2 * span), BF16),
            pltpu.VMEM((pixels, 2 * KSEG * span), BF16),
            pltpu.VMEM((2 * KSEG * span, LANES), BF16),
            pltpu.VMEM((KSEG, pixels, span), F32),
            pltpu.VMEM((KSEG, 2, SIDE, span), F32),
            pltpu.VMEM((KSEG, ROWS, span), F32),
            pltpu.VMEM((pixels, LANES), F32),
            pltpu.VMEM((LANES, slots // 2), F32),
        ],
        compiler_params=PARAMS,
        name="render",
    )(me, order, tri, goal, goal_cols, *blocks)
    hot = pl.pallas_call(
        functools.partial(asked_kernel, cap, base + SUB, ndev, owned),
        out_shape=jax.ShapeDtypeStruct((slots, owned), BF16),
        in_specs=[SMEM] + [VMEM] * len(blocks),
        out_specs=VMEM,
        scratch_shapes=[pltpu.VMEM((slots, LANES), F32)],
        compiler_params=PARAMS,
        name="asked",
    )(me, *blocks)
    grads, hot = lax.optimization_barrier((grads, hot))
    returned = lax.all_to_all(grads, "dev", split_axis=0, concat_axis=0, tiled=True)
    new = jax.ShapeDtypeStruct(params.shape, F32)
    new_params, new_moment, new_second = pl.pallas_call(
        functools.partial(update_kernel, segs, ndev),
        out_shape=(new, new, new),
        in_specs=[SMEM, SMEM] + [VMEM] * 5,
        out_specs=(VMEM, VMEM, VMEM),
        scratch_shapes=[pltpu.VMEM((slots // 2, LANES), F32)],
        compiler_params=PARAMS,
        name="update",
    )(me, seg_perm, returned, hot, params, moment, second)
    return (image.transpose(1, 0, 2), new_params, new_moment, new_second)


def solution(mesh):
    placed = (
        P(None, "dev"),
        P(None, "dev"),
        P(None, "dev"),
        P("dev", None, None),
        P("dev", None),
        P("dev"),
        P(),
        P("dev", None, None),
    )
    return jax.shard_map(
        per_device,
        mesh=mesh,
        in_specs=placed,
        out_specs=(P("dev", None, None), P(None, "dev"), P(None, "dev"), P(None, "dev")),
        check_vma=False,
    )
```

```python
import functools

import jax
import jax.numpy as jnp
from jax import lax
from jax.experimental import pallas as pl
from jax.experimental.pallas import tpu as pltpu
from jax.sharding import PartitionSpec as P

TILES_X = 8
KSEG = 4
SIDE = 16
LANES = 128
SUB = 8
ROWS = 16
F32 = jnp.float32
BF16 = jnp.bfloat16
SMEM = pl.BlockSpec(memory_space=pltpu.SMEM)
VMEM = pl.BlockSpec(memory_space=pltpu.VMEM)
HBM = pl.BlockSpec(memory_space=pltpu.HBM)
PARAMS = pltpu.CompilerParams(vmem_limit_bytes=40 * 2**20)


def split2(x):
    high = x.astype(BF16)
    return high, (x - high.astype(F32)).astype(BF16)


def split3(x):
    high = x.astype(BF16)
    rest = x - high.astype(F32)
    mid = rest.astype(BF16)
    return high, mid, (rest - mid.astype(F32)).astype(BF16)


def iota(shape, dim):
    return lax.broadcasted_iota(jnp.int32, shape, dim)


def dot(a, b, dims=((1,), (0,))):
    return lax.dot_general(a, b, (dims, ((), ())), preferred_element_type=F32)


def stages(ndev):
    top, place, out = ndev.bit_length() - 1, 0, []
    assert ndev == 1 << top and top >= 3
    while top > 1:
        bits = min(2, top - 1)
        top -= bits
        out.append((top, bits, place))
        place += bits
    return out + [(0, 1, place)]


def position(ndev, offset):
    return sum(((offset >> bit) & ((1 << bits) - 1)) << place for bit, bits, place in stages(ndev))


def offset_at(ndev, pos):
    return sum(((pos >> place) & ((1 << bits) - 1)) << bit for bit, bits, place in stages(ndev))


def gather_blocks(block, ndev, beside):
    def pull(x, change):
        return lax.ppermute(x, "dev", [(d, d ^ change) for d in range(ndev)])

    held, steps = [block[None]], stages(ndev)
    for number, (bit, bits, _) in enumerate(steps[:-1]):
        whole = held[0] if len(held) == 1 else jnp.concatenate(held, 0)
        if number == 1:
            whole, beside = lax.optimization_barrier((whole, beside))
        held = [whole] + [pull(whole, change << bit) for change in range(1, 1 << bits)]
    return held + [pull(x, 1) for x in held], beside


def pick(source, lanes):
    return jnp.take_along_axis(source, lanes, axis=1)


def sum_rows(blocks):
    row = iota((SUB, LANES), 0)
    for step in (1, 2, 4):
        first = row & step == 0
        blocks = [
            jnp.where(first, a, b) + pltpu.roll(jnp.where(first, b, a), step, 0)
            for a, b in zip(blocks[::2], blocks[1::2], strict=True)
        ]
    return blocks[0]


def pack_kernel(count_in, seg_in, fetch_in, params_in, out, count, seg, fetch, params, sems):
    segs, span = seg.shape
    nparam, owned = params.shape
    chunks, halves = owned // LANES, span // LANES
    lane = iota((1, LANES), 1)
    pairs = ((params_in, params), (seg_in, seg), (fetch_in, fetch), (count_in, count))
    copies = [pltpu.make_async_copy(a, b, sems.at[i]) for i, (a, b) in enumerate(pairs)]
    for copy in copies:
        copy.start()
    for copy in copies:
        copy.wait()
    for p in range(nparam):
        for c in range(chunks):
            out[p * chunks + c : p * chunks + c + 1, :] = params[p : p + 1, c * LANES : (c + 1) * LANES]
    at = nparam * chunks
    for s in range(segs):
        for h in range(halves):
            row = jnp.where(lane + h * LANES < count[s], seg[s : s + 1, h * LANES : (h + 1) * LANES], -1)
            out[at : at + 1, :] = row.astype(F32)
            at += 1
    out[at : at + SUB, :] = jnp.zeros((SUB, LANES), F32)
    out[at : at + SUB, : fetch.shape[1]] = fetch[...].astype(F32)


def layout_kernel(me_ref, perm, target, tri, goal, goal_cols, back):
    width = back.shape[1]
    ndev = width // 4
    lane = iota((SUB, LANES), 1)
    row = iota((KSEG * width, LANES), 0)
    wanted = ((row & (width - 1)) >> 2) * KSEG + row // width
    for part in range(width // LANES):
        cols = lane + part * LANES
        requester = offset_at(ndev, cols >> 2) ^ me_ref[0]
        same_k = (iota((KSEG * width, LANES), 1) & 3) == (row & 3)
        hit = jnp.zeros((KSEG * width, LANES), F32)
        for s in range(KSEG):
            at = requester * KSEG + s
            held = jnp.zeros((SUB, LANES), F32)
            for g in range(perm.shape[0]):
                source = jnp.broadcast_to(perm[g : g + 1, :].astype(F32), (SUB, LANES))
                held = jnp.where(at >> 7 == g, pick(source, at & (LANES - 1)), held)
            held = held[:1, :].astype(jnp.int32)
            hit = hit + jnp.where((wanted == held) & same_k, 1.0, 0.0)
        back[:, part * LANES : (part + 1) * LANES] = hit.astype(BF16)
    span = tri.shape[2]
    src, dst = iota((span, span), 0), iota((span, span), 1)
    before = (src < dst).astype(F32).astype(BF16)
    after = (src > dst).astype(F32).astype(BF16)
    for half in range(2):
        tri[0, half * span : (half + 1) * span, :] = before
        tri[1, half * span : (half + 1) * span, :] = after
    rows = jnp.concatenate([target[c] for c in range(3)], 0)
    pixels = rows.shape[1]
    wide = jnp.concatenate([rows] * 3 + [jnp.zeros((LANES - 9, pixels), F32)], 0)
    goal[...] = wide[:ROWS]
    goal_cols[...] = wide.T


def render_kernel(segs, cap, nparam, chunks, ndev, *refs):
    me_ref, perm, tri, goal, goal_cols = refs[:5]
    narr = 2 << stages(ndev)[-2][1]
    arrays = refs[5 : 5 + narr]
    image, grads, asked = refs[5 + narr : 8 + narr]
    (column, ids, lists, idrows, table, hots, coef, alpha, trans, logs, weights, colours, backs, dys, dpar, gback, flat) = refs[8 + narr :]
    per = arrays[0].shape[0]
    slots = ndev * cap
    quarter = slots // 2
    pixels = SIDE * SIDE
    span = hots.shape[1]
    halves = span // LANES
    me = me_ref[0]
    base = nparam * chunks

    def block(j):
        return arrays[j // per], j % per

    for j in range(ndev):
        ref, at = block(j)
        idrows[j] = ref[at, base : base + 2 * SUB, :]
    fetched = []
    places = (iota(perm.shape, 0) * LANES + iota(perm.shape, 1)).astype(F32)
    for q in range(KSEG):
        slot = jnp.sum(jnp.where(perm[...] == me * KSEG + q, places, 0.0)).astype(jnp.int32)
        j = position(ndev, (slot >> 2) ^ me)
        fetched.append(idrows[j, SUB : 2 * SUB, :])
        for h in range(halves):
            lists[q * halves + h : q * halves + h + 1, :] = idrows[j, pl.ds((slot & 3) * halves + h, 1), :]
    sub, lane = iota((SUB, LANES), 0), iota((SUB, LANES), 1)
    low_bits = cap.bit_length() - 1
    rank, which = (lane >> low_bits) & (KSEG - 1), lane >> (low_bits + 2)
    extra = []
    for g in range(ndev // 4):
        offs = [offset_at(ndev, 4 * g + b) for b in range(4)]
        off = jnp.where(which == 0, offs[0], jnp.where(which == 1, offs[1], jnp.where(which == 2, offs[2], offs[3])))
        owner = off ^ me
        found = jnp.zeros((SUB, LANES), F32)
        for q in range(KSEG):
            found = jnp.where(rank == q, pick(fetched[q], owner), found)
        found = jnp.where(sub == lane & (cap - 1), found, 0.0)
        for step in (4, 2, 1):
            found = found + pltpu.roll(found, step, 0)
        local = found.astype(jnp.int32)
        inside, chunk = local & (LANES - 1), local >> 7
        got = []
        for p in range(nparam):
            value = jnp.zeros((SUB, LANES), F32)
            for b in range(4):
                ref, at = block(4 * g + b)
                value = jnp.where(which == b, pick(ref[at, p * chunks : (p + 1) * chunks, :], inside), value)
            got.append(jnp.where(sub == chunk, value, 0.0))
        table[g] = sum_rows(got[:SUB])
        last = got[SUB]
        for step in (4, 2, 1):
            last = last + pltpu.roll(last, step, 0)
        extra.append(last)
    listed = lists[...].astype(jnp.int32)
    slot = jnp.maximum(listed, 0)
    pos = position(ndev, (slot >> low_bits) ^ me)
    spot = ((pos & 3) << (low_bits + 2)) + ((sub // halves) << low_bits) + (slot & (cap - 1))
    team = pos >> 2
    live = listed >= 0
    ninth = jnp.zeros((SUB, LANES), F32)
    for g in range(ndev // 4):
        ninth = jnp.where(team == g, pick(extra[g], spot), ninth)
    ninth = jnp.where(live, ninth, 0.0)
    k = slot & (cap - 1)
    into = jnp.where(live, (k >> 2) * quarter + (slot >> low_bits) * 4 + (k & 3), -1).astype(F32)
    for q in range(KSEG):
        for h in range(halves):
            row = q * halves + h
            cols = slice(h * LANES, (h + 1) * LANES)
            spot_row = jnp.broadcast_to(spot[row : row + 1, :], (SUB, LANES))
            team_row = jnp.broadcast_to(team[row : row + 1, :], (SUB, LANES))
            value = jnp.zeros((SUB, LANES), F32)
            for g in range(ndev // 4):
                value = jnp.where(team_row == g, pick(table[g], spot_row), value)
            coef[q, :SUB, cols] = jnp.where(live[row : row + 1, :], value, 0.0)
            coef[q, SUB : SUB + 1, cols] = ninth[row : row + 1, :]
            ids[q : q + 1, cols] = into[row : row + 1, :]
    thin = iota((span, LANES), 1)
    gap = jnp.zeros((ROWS - 9, span), F32)
    groups = []
    for q in range(KSEG):
        hi, mid = split2(coef[q, 6:9, :])
        groups += [hi.astype(F32)] * 3 + [gap] + [mid.astype(F32)] * 3 + [gap]
    columns = jnp.concatenate(groups, 0).T
    for q in range(KSEG):
        both = pltpu.roll(columns, LANES - 2 * q * ROWS, 1) if q else columns
        colours[2 * q * span : (2 * q + 1) * span, :] = jnp.where(thin < 2 * ROWS, both, 0.0).astype(BF16)
        colours[(2 * q + 1) * span : 2 * (q + 1) * span, :] = jnp.where(thin < ROWS, both, 0.0).astype(BF16)
    slot_lane = iota((span, slots), 1)
    fine = (iota((SIDE, span), 0).astype(F32) + 0.5) / SIDE
    pos_x = (me % TILES_X).astype(F32) + fine
    pos_y = (me // TILES_X).astype(F32) + fine

    par, dxs = [], []
    for q in range(KSEG):
        alive = (ids[q : q + 1, :] >= 0.0).astype(F32)
        got = coef[q]
        mx, my = got[0:1], got[1:2]
        ex, ey = jnp.exp(got[2:3]), jnp.exp(got[3:4])
        th = jnp.tanh(got[4:5])
        sa, sc, cross = ex * ex, ey * ey, 0.8 * th * ex * ey
        peak = 0.95 / (1.0 + jnp.exp(-got[5:6])) * alive
        dx = pos_x - mx
        dy = pos_y - my
        xa = -0.5 * sa * dx * dx
        xb = -cross * dx
        dys[q, 0] = dy
        dys[q, 1] = -0.5 * sc * dy * dy
        par.append((sa, sc, cross, ex, ey, th))
        dxs.append(dx)
        for y in range(SIDE):
            power = xa + dys[q, 0, y : y + 1, :] * xb + dys[q, 1, y : y + 1, :]
            al = peak * jnp.exp(power)
            at = slice(y * SIDE, (y + 1) * SIDE)
            alpha[q, at, :] = al
            hi, mid = split2(jnp.log(1.0 - al))
            logs[q, at, :span] = hi
            logs[q, at, span:] = mid
        trans[q] = dot(logs[q], tri[0])

    rows_of = ids[...].T.astype(jnp.int32)
    for q in range(KSEG):
        hots[q] = (slot_lane == rows_of[:, q : q + 1]).astype(F32).astype(BF16)
    ahead = jnp.zeros((pixels, 1), F32)
    lane = iota((pixels, LANES), 1)
    for q in range(KSEG):
        gback[...] = jnp.broadcast_to(ahead, (pixels, LANES))
        ahead = ahead + trans[q, :, span - 1 : span] + jnp.log(1.0 - alpha[q, :, span - 1 : span])
        for y in range(SIDE):
            at = slice(y * SIDE, (y + 1) * SIDE)
            both = jnp.concatenate([gback[at, :]] * halves, 1)
            t = jnp.exp(trans[q, at, :] + both)
            trans[q, at, :] = t
            hi, mid = split2(t * alpha[q, at, :])
            weights[at, 2 * q * span : (2 * q + 1) * span] = hi
            weights[at, (2 * q + 1) * span : 2 * (q + 1) * span] = mid
    shown = dot(weights[...], colours[...])
    e_hi, e_mid = split2(shown - goal_cols[...])
    e_cols = jnp.where((lane < 6) | (lane >= 9), e_hi.astype(F32), e_mid.astype(F32)).astype(BF16)
    shot = shown.T
    shot = shot[:ROWS] + shot[ROWS : 2 * ROWS]
    for c in range(3):
        image[c] = shot[c : c + 1, :]
    er_both = jnp.concatenate(split2(shot - goal[...]), 0)
    for j in range(ndev):
        column[4 * j : 4 * j + 4, :] = idrows[j, SUB : SUB + 4, :]
        column[quarter + 4 * j : quarter + 4 * j + 4, :] = idrows[j, SUB + 4 : 2 * SUB, :]
    mine = iota(column.shape, 1) == me
    wanted = jnp.sum(jnp.where(mine, column[...], 0.0), 1, keepdims=True).astype(jnp.int32)
    for c in range(chunks):
        cols = iota(column.shape, 1) + c * LANES
        asked[:, c * LANES : (c + 1) * LANES] = (wanted == cols).astype(F32).astype(BF16)
    behind = jnp.zeros((pixels, 1), F32)
    for q in range(KSEG):
        hi, mid = split2(coef[q, 6:9, :])
        hi, mid = hi.astype(F32), mid.astype(F32)
        gap = jnp.zeros((ROWS - 9, span), F32)
        c_rows = jnp.concatenate([hi, mid, hi, gap, hi, jnp.zeros((LANES - ROWS - 3, span), F32)], 0).astype(BF16)
        slope = dot(e_cols, c_rows)
        dcol = dot(er_both, weights[:, 2 * q * span : (2 * q + 1) * span])
        dcol = dcol[:ROWS] + dcol[ROWS:] + dot(er_both[:ROWS], weights[:, (2 * q + 1) * span : 2 * (q + 1) * span])
        dpar[q, 6:9, :] = dcol[0:3]
        for y in range(SIDE):
            at = slice(y * SIDE, (y + 1) * SIDE)
            gt = slope[at] * trans[q, at, :]
            trans[q, at, :] = gt
            hi, mid = split2(gt * alpha[q, at, :])
            logs[q, at, :span] = hi
            logs[q, at, span:] = mid
        backs[q] = dot(logs[q], tri[1])
    for q in reversed(range(KSEG)):
        gback[...] = jnp.broadcast_to(behind, (pixels, LANES))
        behind = behind + backs[q, :, 0:1] + trans[q, :, 0:1] * alpha[q, :, 0:1]
        sa, sc, cross, ex, ey, th = par[q]
        dx = dxs[q]
        d0 = jnp.zeros((SIDE, span), F32)
        d1 = jnp.zeros((SIDE, span), F32)
        d2 = jnp.zeros((SIDE, span), F32)
        for y in range(SIDE):
            at = slice(y * SIDE, (y + 1) * SIDE)
            both = jnp.concatenate([gback[at, :]] * halves, 1)
            al = alpha[q, at, :]
            d = (trans[q, at, :] - (backs[q, at, :] + both) / (1.0 - al)) * al
            ddy = d * dys[q, 0, y : y + 1, :]
            d0 = d0 + d
            d1 = d1 + ddy
            d2 = d2 + ddy * dys[q, 0, y : y + 1, :]
        m0 = jnp.sum(d0, 0, keepdims=True)
        m_x = jnp.sum(d0 * dx, 0, keepdims=True)
        m_y = jnp.sum(d1, 0, keepdims=True)
        m_xx = jnp.sum(d0 * dx * dx, 0, keepdims=True)
        m_xy = jnp.sum(d1 * dx, 0, keepdims=True)
        m_yy = jnp.sum(d2, 0, keepdims=True)
        dpar[q, 0:1, :] = sa * m_x + cross * m_y
        dpar[q, 1:2, :] = cross * m_x + sc * m_y
        dpar[q, 2:3, :] = -(sa * m_xx + cross * m_xy)
        dpar[q, 3:4, :] = -(sc * m_yy + cross * m_xy)
        dpar[q, 4:5, :] = -0.8 * (1.0 - th) * (1.0 + th) * ex * ey * m_xy
        dpar[q, 5:6, :] = m0 / (1.0 + jnp.exp(coef[q, 5:6, :]))
        dpar[q, nparam:, :] = jnp.zeros((ROWS - nparam, span), F32)
        parts = jnp.concatenate(split3(dpar[q]), 0)
        back = dot(parts, hots[q])
        back = back[:ROWS] + back[ROWS : 2 * ROWS] + back[2 * ROWS :]
        for half in range(2):
            row = half * KSEG * ROWS + q * ROWS
            flat[row : row + ROWS, :] = back[:, half * quarter : (half + 1) * quarter]
    turned = flat[...].T
    for o in range(ndev):
        grads[o] = turned[4 * o : 4 * o + 4, :]


def update_kernel(returned, back, hot, params, moment, second, new_params, new_moment, new_second):
    nparam = params.shape[0]
    flat = returned[...].T
    half = KSEG * ROWS
    sides = [
        jnp.concatenate([flat[h * half + q * ROWS : h * half + (q + 1) * ROWS] for q in range(KSEG)], 1)
        for h in range(2)
    ]
    parts = jnp.concatenate(split3(jnp.concatenate(sides, 0)), 0)
    asked = dot(parts, back[...])
    asked = asked[: 2 * ROWS] + asked[2 * ROWS : 4 * ROWS] + asked[4 * ROWS :]
    parts = jnp.concatenate(split3(jnp.concatenate([asked[:ROWS], asked[ROWS:]], 1)), 0)
    grad = dot(parts, hot[...])
    grad = (grad[:ROWS] + grad[ROWS : 2 * ROWS] + grad[2 * ROWS :])[:nparam]
    m = 0.9 * moment[...] + 0.1 * grad
    v = 0.99 * second[...] + 0.01 * grad * grad
    new_moment[...] = m
    new_second[...] = v
    new_params[...] = params[...] - 0.05 * m / (jnp.sqrt(v) + 1e-08)


def per_device(params, moment, second, fetch_ids, seg_ids, seg_count, seg_perm, target):
    ndev = lax.axis_size("dev")
    nparam, owned = params.shape
    segs, span = seg_ids.shape
    cap = fetch_ids.shape[2]
    pixels = target.shape[2]
    slots = ndev * cap
    chunks = owned // LANES
    lists = segs * span // LANES
    assert target.shape[0] == 1 and segs == KSEG and pixels == SIDE * SIDE
    assert cap == SUB and chunks == SUB and lists == SUB and ndev <= LANES and nparam == SUB + 1
    base = nparam * chunks
    perm = seg_perm.reshape(-1, LANES)
    me = lax.axis_index("dev").astype(jnp.int32).reshape(1)

    in_hbm = functools.partial(pltpu.with_memory_space_constraint, memory_space=pltpu.HBM)

    packed = pl.pallas_call(
        pack_kernel,
        out_shape=jax.ShapeDtypeStruct((base + 2 * SUB, LANES), F32),
        in_specs=[HBM] * 4,
        out_specs=VMEM,
        scratch_shapes=[
            pltpu.SMEM(seg_count.shape, jnp.int32),
            pltpu.VMEM(seg_ids.shape, jnp.int32),
            pltpu.VMEM((cap, ndev), jnp.int32),
            pltpu.VMEM(params.shape, F32),
            pltpu.SemaphoreType.DMA((4,)),
        ],
        compiler_params=PARAMS,
        name="pack",
    )(*[in_hbm(x) for x in (seg_count, seg_ids, fetch_ids[0].T, params)])
    tri, goal, goal_cols, back = pl.pallas_call(
        layout_kernel,
        out_shape=(
            jax.ShapeDtypeStruct((2, 2 * span, span), BF16),
            jax.ShapeDtypeStruct((ROWS, pixels), F32),
            jax.ShapeDtypeStruct((pixels, LANES), F32),
            jax.ShapeDtypeStruct((KSEG * 4 * ndev, 4 * ndev), BF16),
        ),
        in_specs=[SMEM, VMEM, VMEM],
        out_specs=(VMEM, VMEM, VMEM, VMEM),
        compiler_params=PARAMS,
        cost_estimate=pl.CostEstimate(flops=0, bytes_accessed=4 * 2**20, transcendentals=0),
        name="layout",
    )(me, perm, target.transpose(1, 0, 2))
    blocks, (tri, goal, goal_cols, back) = gather_blocks(packed, ndev, (tri, goal, goal_cols, back))
    image, grads, hot = pl.pallas_call(
        functools.partial(render_kernel, segs, cap, nparam, chunks, ndev),
        out_shape=(
            jax.ShapeDtypeStruct((3, 1, pixels), F32),
            jax.ShapeDtypeStruct((ndev, 4, LANES), F32),
            jax.ShapeDtypeStruct((slots, owned), BF16),
        ),
        in_specs=[SMEM] + [VMEM] * (4 + len(blocks)),
        out_specs=(VMEM, VMEM, VMEM),
        scratch_shapes=[
            pltpu.VMEM((slots, LANES), F32),
            pltpu.VMEM((SUB, span), F32),
            pltpu.VMEM((SUB, LANES), F32),
            pltpu.VMEM((ndev, 2 * SUB, LANES), F32),
            pltpu.VMEM((ndev // 4, SUB, LANES), F32),
            pltpu.VMEM((KSEG, span, slots), BF16),
            pltpu.VMEM((KSEG, ROWS, span), F32),
            pltpu.VMEM((KSEG, pixels, span), F32),
            pltpu.VMEM((KSEG, pixels, span), F32),
            pltpu.VMEM((KSEG, pixels, 2 * span), BF16),
            pltpu.VMEM((pixels, 2 * KSEG * span), BF16),
            pltpu.VMEM((2 * KSEG * span, LANES), BF16),
            pltpu.VMEM((KSEG, pixels, span), F32),
            pltpu.VMEM((KSEG, 2, SIDE, span), F32),
            pltpu.VMEM((KSEG, ROWS, span), F32),
            pltpu.VMEM((pixels, LANES), F32),
            pltpu.VMEM((LANES, slots // 2), F32),
        ],
        compiler_params=PARAMS,
        name="render",
    )(me, perm, tri, goal, goal_cols, *blocks)
    returned = lax.all_to_all(grads, "dev", split_axis=0, concat_axis=0, tiled=True)
    new = jax.ShapeDtypeStruct(params.shape, F32)
    new_params, new_moment, new_second = pl.pallas_call(
        update_kernel,
        out_shape=(new, new, new),
        in_specs=[VMEM] * 6,
        out_specs=(VMEM, VMEM, VMEM),
        compiler_params=PARAMS,
        name="update",
    )(returned.reshape(4 * ndev, LANES), back, hot, params, moment, second)
    return (image.transpose(1, 0, 2), new_params, new_moment, new_second)


def solution(mesh):
    placed = (
        P(None, "dev"),
        P(None, "dev"),
        P(None, "dev"),
        P("dev", None, None),
        P("dev", None),
        P("dev"),
        P(),
        P("dev", None, None),
    )
    return jax.shard_map(
        per_device,
        mesh=mesh,
        in_specs=placed,
        out_specs=(P("dev", None, None), P(None, "dev"), P(None, "dev"), P(None, "dev")),
        check_vma=False,
    )
```

```python
import functools

import jax
import jax.numpy as jnp
from jax import lax
from jax.experimental import pallas as pl
from jax.experimental.pallas import tpu as pltpu
from jax.sharding import PartitionSpec as P

TILES_X = 8
KSEG = 4
SIDE = 16
LANES = 128
SUB = 8
ROWS = 16
F32 = jnp.float32
BF16 = jnp.bfloat16
SMEM = pl.BlockSpec(memory_space=pltpu.SMEM)
VMEM = pl.BlockSpec(memory_space=pltpu.VMEM)
HBM = pl.BlockSpec(memory_space=pltpu.HBM)
PARAMS = pltpu.CompilerParams(vmem_limit_bytes=40 * 2**20)


def split2(x):
    high = x.astype(BF16)
    return high, (x - high.astype(F32)).astype(BF16)


def split3(x):
    high = x.astype(BF16)
    rest = x - high.astype(F32)
    mid = rest.astype(BF16)
    return high, mid, (rest - mid.astype(F32)).astype(BF16)


def iota(shape, dim):
    return lax.broadcasted_iota(jnp.int32, shape, dim)


def dot(a, b, dims=((1,), (0,))):
    return lax.dot_general(a, b, (dims, ((), ())), preferred_element_type=F32)


def stages(ndev):
    top, place, out = ndev.bit_length() - 1, 0, []
    assert ndev == 1 << top and top >= 3
    while top > 1:
        bits = min(2, top - 1)
        top -= bits
        out.append((top, bits, place))
        place += bits
    return out + [(0, 1, place)]


def position(ndev, offset):
    return sum(((offset >> bit) & ((1 << bits) - 1)) << place for bit, bits, place in stages(ndev))


def offset_at(ndev, pos):
    return sum(((pos >> place) & ((1 << bits) - 1)) << bit for bit, bits, place in stages(ndev))


def gather_blocks(block, ndev, main, beside):
    def pull(x, change):
        return lax.ppermute(x, "dev", [(d, d ^ change) for d in range(ndev)])

    held, steps = [block], stages(ndev)
    for number, (bit, bits, _) in enumerate(steps[:-1]):
        whole = block
        if number == 1:
            held[-1], beside = lax.optimization_barrier((held[-1], beside))
            whole = pl.pallas_call(
                functools.partial(stack_kernel, main),
                out_shape=jax.ShapeDtypeStruct((len(held) * block.shape[0], LANES), F32),
                in_specs=[VMEM] * len(held),
                out_specs=VMEM,
                compiler_params=PARAMS,
                name="stack",
            )(*held)
        elif number:
            whole = jnp.concatenate(held, 0)
        held = [whole] + [pull(whole, change << bit) for change in range(1, 1 << bits)]
    return held + [pull(x, 1) for x in held], beside


def stack_kernel(main, *refs):
    *blocks, out = refs
    rows = blocks[0].shape[0]
    for i, block in enumerate(blocks):
        out[i * main : (i + 1) * main, :] = block[:main, :]
        at = len(blocks) * main + i * (rows - main)
        out[at : at + rows - main, :] = block[main:, :]


def pick(source, lanes):
    return jnp.take_along_axis(source, lanes, axis=1)


def sum_rows(blocks):
    row = iota((SUB, LANES), 0)
    for step in (1, 2, 4):
        first = row & step == 0
        blocks = [
            jnp.where(first, a, b) + pltpu.roll(jnp.where(first, b, a), step, 0)
            for a, b in zip(blocks[::2], blocks[1::2], strict=True)
        ]
    return blocks[0]


def pack_kernel(count_in, seg_in, fetch_in, params_in, out, count, seg, short, fetch, params, sems):
    segs, span = seg.shape
    nparam, owned = params.shape
    chunks, halves = owned // LANES, span // LANES
    lane = iota((1, LANES), 1)
    pairs = ((params_in, params), (seg_in, seg), (fetch_in, short), (count_in, count))
    copies = [pltpu.make_async_copy(a, b, sems.at[i]) for i, (a, b) in enumerate(pairs)]
    for copy in copies:
        copy.start()
    for copy in copies:
        copy.wait()
    for p in range(nparam):
        for c in range(chunks):
            out[p * chunks + c : p * chunks + c + 1, :] = params[p : p + 1, c * LANES : (c + 1) * LANES]
    at = nparam * chunks
    for s in range(segs):
        for h in range(halves):
            row = jnp.where(lane + h * LANES < count[s], seg[s : s + 1, h * LANES : (h + 1) * LANES], -1)
            out[at : at + 1, :] = row.astype(F32)
            at += 1
    ndev = fetch_in.shape[1]
    rows = SUB * ndev // LANES
    if ndev == LANES:
        out[at : at + SUB, :] = short[...].astype(F32)
        return
    fetch[...] = jnp.zeros(fetch.shape, F32)
    fetch[:, :ndev] = short[...].astype(F32)
    lane, sub = iota((SUB, LANES), 1), iota((SUB, LANES), 0)
    wide = pick(fetch[...], lane & (ndev - 1))
    for r in range(rows):
        own = jnp.where(sub == r * (SUB // rows) + lane // ndev, wide, 0.0)
        out[at + r : at + r + 1, :] = jnp.sum(own, 0, keepdims=True)


def layout_kernel(me_ref, perm, target, tri, goal, goal_cols, back):
    width = back.shape[1]
    ndev = width // 4
    lane = iota((SUB, LANES), 1)
    row = iota((KSEG * width, LANES), 0)
    wanted = ((row & (width - 1)) >> 2) * KSEG + row // width
    for part in range(width // LANES):
        cols = lane + part * LANES
        requester = offset_at(ndev, cols >> 2) ^ me_ref[0]
        same_k = (iota((KSEG * width, LANES), 1) & 3) == (row & 3)
        hit = jnp.zeros((KSEG * width, LANES), F32)
        for s in range(KSEG):
            at = requester * KSEG + s
            held = jnp.zeros((SUB, LANES), F32)
            for g in range(perm.shape[0]):
                source = jnp.broadcast_to(perm[g : g + 1, :].astype(F32), (SUB, LANES))
                held = jnp.where(at >> 7 == g, pick(source, at & (LANES - 1)), held)
            held = held[:1, :].astype(jnp.int32)
            hit = hit + jnp.where((wanted == held) & same_k, 1.0, 0.0)
        back[:, part * LANES : (part + 1) * LANES] = hit.astype(BF16)
    span = tri.shape[2]
    src, dst = iota((span, span), 0), iota((span, span), 1)
    before = (src < dst).astype(F32).astype(BF16)
    after = (src > dst).astype(F32).astype(BF16)
    for half in range(2):
        tri[0, half * span : (half + 1) * span, :] = before
        tri[1, half * span : (half + 1) * span, :] = after
    rows = jnp.concatenate([target[c] for c in range(3)], 0)
    pixels = rows.shape[1]
    wide = jnp.concatenate([rows] * 3 + [jnp.zeros((LANES - 9, pixels), F32)], 0)
    goal[...] = wide[:ROWS]
    goal_cols[...] = wide.T


def render_kernel(segs, cap, nparam, chunks, ndev, *refs):
    me_ref, perm, tri, goal, goal_cols = refs[:5]
    narr = 2 << stages(ndev)[-2][1]
    arrays = refs[5 : 5 + narr]
    image, grads, asked = refs[5 + narr : 8 + narr]
    (column, ids, lists, idrows, table, hots, coef, alpha, trans, logs, weights, colours, backs, dys, dpar, gback, flat) = refs[8 + narr :]
    main, tail = nparam * chunks + SUB, SUB * ndev // LANES
    unit = 4 * (main + tail)
    per = arrays[0].shape[0] * 4 // unit
    slots = ndev * cap
    quarter = slots // 2
    pixels = SIDE * SIDE
    span = hots.shape[1]
    halves = span // LANES
    me = me_ref[0]
    base = nparam * chunks

    def block(j):
        return arrays[j // per], j % per // 4 * unit + j % 4 * main

    for j in range(ndev):
        ref, at = block(j)
        idrows[j, :SUB, :] = ref[at + base : at + base + SUB, :]
        at = j % per // 4 * unit + 4 * main + j % 4 * tail
        idrows[j, SUB : SUB + tail, :] = ref[at : at + tail, :]
    fetched = []
    places = (iota(perm.shape, 0) * LANES + iota(perm.shape, 1)).astype(F32)
    for q in range(KSEG):
        slot = jnp.sum(jnp.where(perm[...] == me * KSEG + q, places, 0.0)).astype(jnp.int32)
        j = position(ndev, (slot >> 2) ^ me)
        fetched.append([jnp.broadcast_to(idrows[j, SUB + r : SUB + r + 1, :], (SUB, LANES)) for r in range(tail)])
        for h in range(halves):
            lists[q * halves + h : q * halves + h + 1, :] = idrows[j, pl.ds((slot & 3) * halves + h, 1), :]
    sub, lane = iota((SUB, LANES), 0), iota((SUB, LANES), 1)
    low_bits = cap.bit_length() - 1
    rank, which = (lane >> low_bits) & (KSEG - 1), lane >> (low_bits + 2)
    kth, share = lane & (cap - 1), SUB // tail
    extra = []
    for g in range(ndev // 4):
        offs = [offset_at(ndev, 4 * g + b) for b in range(4)]
        off = jnp.where(which == 0, offs[0], jnp.where(which == 1, offs[1], jnp.where(which == 2, offs[2], offs[3])))
        owner = off ^ me
        found = jnp.zeros((SUB, LANES), F32)
        source = (kth & (share - 1)) * ndev + owner
        for r in range(tail):
            here = jnp.zeros((SUB, LANES), F32)
            for q in range(KSEG):
                here = jnp.where(rank == q, pick(fetched[q][r], source), here)
            found = jnp.where(kth // share == r, here, found)
        local = found.astype(jnp.int32)
        inside, chunk = local & (LANES - 1), local >> 7
        got = []
        for p in range(nparam):
            value = jnp.zeros((SUB, LANES), F32)
            for b in range(4):
                ref, at = block(4 * g + b)
                value = jnp.where(which == b, pick(ref[at + p * chunks : at + (p + 1) * chunks, :], inside), value)
            got.append(jnp.where(sub == chunk, value, 0.0))
        table[g] = sum_rows(got[:SUB])
        last = got[SUB]
        for step in (4, 2, 1):
            last = last + pltpu.roll(last, step, 0)
        extra.append(last)
    listed = lists[...].astype(jnp.int32)
    slot = jnp.maximum(listed, 0)
    pos = position(ndev, (slot >> low_bits) ^ me)
    spot = ((pos & 3) << (low_bits + 2)) + ((sub // halves) << low_bits) + (slot & (cap - 1))
    team = pos >> 2
    live = listed >= 0
    ninth = jnp.zeros((SUB, LANES), F32)
    for g in range(ndev // 4):
        ninth = jnp.where(team == g, pick(extra[g], spot), ninth)
    ninth = jnp.where(live, ninth, 0.0)
    k = slot & (cap - 1)
    into = jnp.where(live, (k >> 2) * quarter + (slot >> low_bits) * 4 + (k & 3), -1).astype(F32)
    for q in range(KSEG):
        for h in range(halves):
            row = q * halves + h
            cols = slice(h * LANES, (h + 1) * LANES)
            spot_row = jnp.broadcast_to(spot[row : row + 1, :], (SUB, LANES))
            team_row = jnp.broadcast_to(team[row : row + 1, :], (SUB, LANES))
            value = jnp.zeros((SUB, LANES), F32)
            for g in range(ndev // 4):
                value = jnp.where(team_row == g, pick(table[g], spot_row), value)
            coef[q, :SUB, cols] = jnp.where(live[row : row + 1, :], value, 0.0)
            coef[q, SUB : SUB + 1, cols] = ninth[row : row + 1, :]
            ids[q : q + 1, cols] = into[row : row + 1, :]
    thin = iota((span, LANES), 1)
    gap = jnp.zeros((ROWS - 9, span), F32)
    groups = []
    for q in range(KSEG):
        hi, mid = split2(coef[q, 6:9, :])
        groups += [hi.astype(F32)] * 3 + [gap] + [mid.astype(F32)] * 3 + [gap]
    columns = jnp.concatenate(groups, 0).T
    for q in range(KSEG):
        both = pltpu.roll(columns, LANES - 2 * q * ROWS, 1) if q else columns
        colours[2 * q * span : (2 * q + 1) * span, :] = jnp.where(thin < 2 * ROWS, both, 0.0).astype(BF16)
        colours[(2 * q + 1) * span : 2 * (q + 1) * span, :] = jnp.where(thin < ROWS, both, 0.0).astype(BF16)
    slot_lane = iota((span, slots), 1)
    fine = (iota((SIDE, span), 0).astype(F32) + 0.5) / SIDE
    pos_x = (me % TILES_X).astype(F32) + fine
    pos_y = (me // TILES_X).astype(F32) + fine

    par, dxs = [], []
    for q in range(KSEG):
        alive = (ids[q : q + 1, :] >= 0.0).astype(F32)
        got = coef[q]
        mx, my = got[0:1], got[1:2]
        ex, ey = jnp.exp(got[2:3]), jnp.exp(got[3:4])
        th = jnp.tanh(got[4:5])
        sa, sc, cross = ex * ex, ey * ey, 0.8 * th * ex * ey
        peak = 0.95 / (1.0 + jnp.exp(-got[5:6])) * alive
        dx = pos_x - mx
        dy = pos_y - my
        xa = -0.5 * sa * dx * dx
        xb = -cross * dx
        dys[q, 0] = dy
        dys[q, 1] = -0.5 * sc * dy * dy
        par.append((sa, sc, cross, ex, ey, th))
        dxs.append(dx)
        for y in range(SIDE):
            power = xa + dys[q, 0, y : y + 1, :] * xb + dys[q, 1, y : y + 1, :]
            al = peak * jnp.exp(power)
            at = slice(y * SIDE, (y + 1) * SIDE)
            alpha[q, at, :] = al
            hi, mid = split2(jnp.log(1.0 - al))
            logs[q, at, :span] = hi
            logs[q, at, span:] = mid
        trans[q] = dot(logs[q], tri[0])

    rows_of = ids[...].T.astype(jnp.int32)
    for q in range(KSEG):
        hots[q] = (slot_lane == rows_of[:, q : q + 1]).astype(F32).astype(BF16)
    ahead = jnp.zeros((pixels, 1), F32)
    lane = iota((pixels, LANES), 1)
    for q in range(KSEG):
        gback[...] = jnp.broadcast_to(ahead, (pixels, LANES))
        ahead = ahead + trans[q, :, span - 1 : span] + jnp.log(1.0 - alpha[q, :, span - 1 : span])
        for y in range(SIDE):
            at = slice(y * SIDE, (y + 1) * SIDE)
            both = jnp.concatenate([gback[at, :]] * halves, 1)
            t = jnp.exp(trans[q, at, :] + both)
            trans[q, at, :] = t
            hi, mid = split2(t * alpha[q, at, :])
            weights[at, 2 * q * span : (2 * q + 1) * span] = hi
            weights[at, (2 * q + 1) * span : 2 * (q + 1) * span] = mid
    shown = dot(weights[...], colours[...])
    e_hi, e_mid = split2(shown - goal_cols[...])
    e_cols = jnp.where((lane < 6) | (lane >= 9), e_hi.astype(F32), e_mid.astype(F32)).astype(BF16)
    shot = shown.T
    shot = shot[:ROWS] + shot[ROWS : 2 * ROWS]
    for c in range(3):
        image[c] = shot[c : c + 1, :]
    er_both = jnp.concatenate(split2(shot - goal[...]), 0)
    for j in range(ndev):
        for k in range(cap):
            row = k // 4 * quarter + 4 * j + k % 4
            column[row : row + 1, :] = idrows[j, SUB + k // share : SUB + k // share + 1, :]
    line = iota(column.shape, 0)
    spot_k = jnp.where(line < quarter, 0, 4) + (line & 3)
    mine = iota(column.shape, 1) == (spot_k & (share - 1)) * ndev + me
    wanted = jnp.sum(jnp.where(mine, column[...], 0.0), 1, keepdims=True).astype(jnp.int32)
    for c in range(chunks):
        cols = iota(column.shape, 1) + c * LANES
        asked[:, c * LANES : (c + 1) * LANES] = (wanted == cols).astype(F32).astype(BF16)
    behind = jnp.zeros((pixels, 1), F32)
    for q in range(KSEG):
        hi, mid = split2(coef[q, 6:9, :])
        hi, mid = hi.astype(F32), mid.astype(F32)
        gap = jnp.zeros((ROWS - 9, span), F32)
        c_rows = jnp.concatenate([hi, mid, hi, gap, hi, jnp.zeros((LANES - ROWS - 3, span), F32)], 0).astype(BF16)
        slope = dot(e_cols, c_rows)
        dcol = dot(er_both, weights[:, 2 * q * span : (2 * q + 1) * span])
        dcol = dcol[:ROWS] + dcol[ROWS:] + dot(er_both[:ROWS], weights[:, (2 * q + 1) * span : 2 * (q + 1) * span])
        dpar[q, 6:9, :] = dcol[0:3]
        for y in range(SIDE):
            at = slice(y * SIDE, (y + 1) * SIDE)
            gt = slope[at] * trans[q, at, :]
            trans[q, at, :] = gt
            hi, mid = split2(gt * alpha[q, at, :])
            logs[q, at, :span] = hi
            logs[q, at, span:] = mid
        backs[q] = dot(logs[q], tri[1])
    for q in reversed(range(KSEG)):
        gback[...] = jnp.broadcast_to(behind, (pixels, LANES))
        behind = behind + backs[q, :, 0:1] + trans[q, :, 0:1] * alpha[q, :, 0:1]
        sa, sc, cross, ex, ey, th = par[q]
        dx = dxs[q]
        d0 = jnp.zeros((SIDE, span), F32)
        d1 = jnp.zeros((SIDE, span), F32)
        d2 = jnp.zeros((SIDE, span), F32)
        for y in range(SIDE):
            at = slice(y * SIDE, (y + 1) * SIDE)
            both = jnp.concatenate([gback[at, :]] * halves, 1)
            al = alpha[q, at, :]
            d = (trans[q, at, :] - (backs[q, at, :] + both) / (1.0 - al)) * al
            ddy = d * dys[q, 0, y : y + 1, :]
            d0 = d0 + d
            d1 = d1 + ddy
            d2 = d2 + ddy * dys[q, 0, y : y + 1, :]
        m0 = jnp.sum(d0, 0, keepdims=True)
        m_x = jnp.sum(d0 * dx, 0, keepdims=True)
        m_y = jnp.sum(d1, 0, keepdims=True)
        m_xx = jnp.sum(d0 * dx * dx, 0, keepdims=True)
        m_xy = jnp.sum(d1 * dx, 0, keepdims=True)
        m_yy = jnp.sum(d2, 0, keepdims=True)
        dpar[q, 0:1, :] = sa * m_x + cross * m_y
        dpar[q, 1:2, :] = cross * m_x + sc * m_y
        dpar[q, 2:3, :] = -(sa * m_xx + cross * m_xy)
        dpar[q, 3:4, :] = -(sc * m_yy + cross * m_xy)
        dpar[q, 4:5, :] = -0.8 * (1.0 - th) * (1.0 + th) * ex * ey * m_xy
        dpar[q, 5:6, :] = m0 / (1.0 + jnp.exp(coef[q, 5:6, :]))
        dpar[q, nparam:, :] = jnp.zeros((ROWS - nparam, span), F32)
        parts = jnp.concatenate(split3(dpar[q]), 0)
        back = dot(parts, hots[q])
        back = back[:ROWS] + back[ROWS : 2 * ROWS] + back[2 * ROWS :]
        for half in range(2):
            row = half * KSEG * ROWS + q * ROWS
            flat[row : row + ROWS, :] = back[:, half * quarter : (half + 1) * quarter]
    turned = flat[...].T
    for o in range(ndev):
        grads[o] = turned[4 * o : 4 * o + 4, :]


def update_kernel(returned, back, hot, params, moment, second, new_params, new_moment, new_second):
    nparam = params.shape[0]
    flat = returned[...].T
    half = KSEG * ROWS
    sides = [
        jnp.concatenate([flat[h * half + q * ROWS : h * half + (q + 1) * ROWS] for q in range(KSEG)], 1)
        for h in range(2)
    ]
    parts = jnp.concatenate(split3(jnp.concatenate(sides, 0)), 0)
    asked = dot(parts, back[...])
    asked = asked[: 2 * ROWS] + asked[2 * ROWS : 4 * ROWS] + asked[4 * ROWS :]
    parts = jnp.concatenate(split3(jnp.concatenate([asked[:ROWS], asked[ROWS:]], 1)), 0)
    grad = dot(parts, hot[...])
    grad = (grad[:ROWS] + grad[ROWS : 2 * ROWS] + grad[2 * ROWS :])[:nparam]
    m = 0.9 * moment[...] + 0.1 * grad
    v = 0.99 * second[...] + 0.01 * grad * grad
    new_moment[...] = m
    new_second[...] = v
    new_params[...] = params[...] - 0.05 * m / (jnp.sqrt(v) + 1e-08)


def per_device(params, moment, second, fetch_ids, seg_ids, seg_count, seg_perm, target):
    ndev = lax.axis_size("dev")
    nparam, owned = params.shape
    segs, span = seg_ids.shape
    cap = fetch_ids.shape[2]
    pixels = target.shape[2]
    slots = ndev * cap
    chunks = owned // LANES
    lists = segs * span // LANES
    assert target.shape[0] == 1 and segs == KSEG and pixels == SIDE * SIDE
    assert cap == SUB and chunks == SUB and lists == SUB and ndev <= LANES and nparam == SUB + 1
    base = nparam * chunks
    perm = seg_perm.reshape(-1, LANES)
    me = lax.axis_index("dev").astype(jnp.int32).reshape(1)

    in_hbm = functools.partial(pltpu.with_memory_space_constraint, memory_space=pltpu.HBM)

    packed = pl.pallas_call(
        pack_kernel,
        out_shape=jax.ShapeDtypeStruct((base + SUB + slots // LANES, LANES), F32),
        in_specs=[HBM] * 4,
        out_specs=VMEM,
        scratch_shapes=[
            pltpu.SMEM(seg_count.shape, jnp.int32),
            pltpu.VMEM(seg_ids.shape, jnp.int32),
            pltpu.VMEM((cap, ndev), jnp.int32),
            pltpu.VMEM((cap, LANES), F32),
            pltpu.VMEM(params.shape, F32),
            pltpu.SemaphoreType.DMA((4,)),
        ],
        compiler_params=PARAMS,
        name="pack",
    )(*[in_hbm(x) for x in (seg_count, seg_ids, fetch_ids[0].T, params)])
    tri, goal, goal_cols, back = pl.pallas_call(
        layout_kernel,
        out_shape=(
            jax.ShapeDtypeStruct((2, 2 * span, span), BF16),
            jax.ShapeDtypeStruct((ROWS, pixels), F32),
            jax.ShapeDtypeStruct((pixels, LANES), F32),
            jax.ShapeDtypeStruct((KSEG * 4 * ndev, 4 * ndev), BF16),
        ),
        in_specs=[SMEM, VMEM, VMEM],
        out_specs=(VMEM, VMEM, VMEM, VMEM),
        compiler_params=PARAMS,
        cost_estimate=pl.CostEstimate(flops=0, bytes_accessed=4 * 2**20, transcendentals=0),
        name="layout",
    )(me, perm, target.transpose(1, 0, 2))
    blocks, (tri, goal, goal_cols, back) = gather_blocks(packed, ndev, base + SUB, (tri, goal, goal_cols, back))
    image, grads, hot = pl.pallas_call(
        functools.partial(render_kernel, segs, cap, nparam, chunks, ndev),
        out_shape=(
            jax.ShapeDtypeStruct((3, 1, pixels), F32),
            jax.ShapeDtypeStruct((ndev, 4, LANES), F32),
            jax.ShapeDtypeStruct((slots, owned), BF16),
        ),
        in_specs=[SMEM] + [VMEM] * (4 + len(blocks)),
        out_specs=(VMEM, VMEM, VMEM),
        scratch_shapes=[
            pltpu.VMEM((slots, LANES), F32),
            pltpu.VMEM((SUB, span), F32),
            pltpu.VMEM((SUB, LANES), F32),
            pltpu.VMEM((ndev, 2 * SUB, LANES), F32),
            pltpu.VMEM((ndev // 4, SUB, LANES), F32),
            pltpu.VMEM((KSEG, span, slots), BF16),
            pltpu.VMEM((KSEG, ROWS, span), F32),
            pltpu.VMEM((KSEG, pixels, span), F32),
            pltpu.VMEM((KSEG, pixels, span), F32),
            pltpu.VMEM((KSEG, pixels, 2 * span), BF16),
            pltpu.VMEM((pixels, 2 * KSEG * span), BF16),
            pltpu.VMEM((2 * KSEG * span, LANES), BF16),
            pltpu.VMEM((KSEG, pixels, span), F32),
            pltpu.VMEM((KSEG, 2, SIDE, span), F32),
            pltpu.VMEM((KSEG, ROWS, span), F32),
            pltpu.VMEM((pixels, LANES), F32),
            pltpu.VMEM((LANES, slots // 2), F32),
        ],
        compiler_params=PARAMS,
        name="render",
    )(me, perm, tri, goal, goal_cols, *blocks)
    returned = lax.all_to_all(grads, "dev", split_axis=0, concat_axis=0, tiled=True)
    new = jax.ShapeDtypeStruct(params.shape, F32)
    new_params, new_moment, new_second = pl.pallas_call(
        update_kernel,
        out_shape=(new, new, new),
        in_specs=[VMEM] * 6,
        out_specs=(VMEM, VMEM, VMEM),
        compiler_params=PARAMS,
        name="update",
    )(returned.reshape(4 * ndev, LANES), back, hot, params, moment, second)
    return (image.transpose(1, 0, 2), new_params, new_moment, new_second)


def solution(mesh):
    placed = (
        P(None, "dev"),
        P(None, "dev"),
        P(None, "dev"),
        P("dev", None, None),
        P("dev", None),
        P("dev"),
        P(),
        P("dev", None, None),
    )
    return jax.shard_map(
        per_device,
        mesh=mesh,
        in_specs=placed,
        out_specs=(P("dev", None, None), P(None, "dev"), P(None, "dev"), P(None, "dev")),
        check_vma=False,
    )
```

```python
import functools

import jax
import jax.numpy as jnp
from jax import lax
from jax.experimental import pallas as pl
from jax.experimental.pallas import tpu as pltpu
from jax.sharding import PartitionSpec as P

TILES_X = 8
KSEG = 4
SIDE = 16
LANES = 128
SUB = 8
ROWS = 16
F32 = jnp.float32
BF16 = jnp.bfloat16
SMEM = pl.BlockSpec(memory_space=pltpu.SMEM)
VMEM = pl.BlockSpec(memory_space=pltpu.VMEM)
HBM = pl.BlockSpec(memory_space=pltpu.HBM)
PARAMS = pltpu.CompilerParams(vmem_limit_bytes=40 * 2**20)


def split2(x):
    high = x.astype(BF16)
    return high, (x - high.astype(F32)).astype(BF16)


def split3(x):
    high = x.astype(BF16)
    rest = x - high.astype(F32)
    mid = rest.astype(BF16)
    return high, mid, (rest - mid.astype(F32)).astype(BF16)


def iota(shape, dim):
    return lax.broadcasted_iota(jnp.int32, shape, dim)


def dot(a, b, dims=((1,), (0,))):
    return lax.dot_general(a, b, (dims, ((), ())), preferred_element_type=F32)


def stages(ndev):
    top, place, out = ndev.bit_length() - 1, 0, []
    assert ndev == 1 << top and top >= 3
    while top > 1:
        bits = min(2, top - 1)
        top -= bits
        out.append((top, bits, place))
        place += bits
    return out + [(0, 1, place)]


def position(ndev, offset):
    return sum(((offset >> bit) & ((1 << bits) - 1)) << place for bit, bits, place in stages(ndev))


def offset_at(ndev, pos):
    return sum(((pos >> place) & ((1 << bits) - 1)) << bit for bit, bits, place in stages(ndev))


def gather_blocks(block, ndev, main, beside):
    def pull(x, change):
        return lax.ppermute(x, "dev", [(d, d ^ change) for d in range(ndev)])

    held, steps = [block], stages(ndev)
    for number, (bit, bits, _) in enumerate(steps[:-1]):
        whole = block
        if number == 1:
            held[-1], beside = lax.optimization_barrier((held[-1], beside))
            whole = pl.pallas_call(
                functools.partial(stack_kernel, main),
                out_shape=jax.ShapeDtypeStruct((len(held) * block.shape[0], LANES), F32),
                in_specs=[VMEM] * len(held),
                out_specs=VMEM,
                compiler_params=PARAMS,
                name="stack",
            )(*held)
        elif number:
            whole = jnp.concatenate(held, 0)
        held = [whole] + [pull(whole, change << bit) for change in range(1, 1 << bits)]
    return held + [pull(x, 1) for x in held], beside


def stack_kernel(main, *refs):
    *blocks, out = refs
    rows = blocks[0].shape[0]
    for i, block in enumerate(blocks):
        out[i * main : (i + 1) * main, :] = block[:main, :]
        at = len(blocks) * main + i * (rows - main)
        out[at : at + rows - main, :] = block[main:, :]


def pick(source, lanes):
    return jnp.take_along_axis(source, lanes, axis=1)


def sum_rows(blocks):
    row = iota((SUB, LANES), 0)
    for step in (1, 2, 4):
        first = row & step == 0
        blocks = [
            jnp.where(first, a, b) + pltpu.roll(jnp.where(first, b, a), step, 0)
            for a, b in zip(blocks[::2], blocks[1::2], strict=True)
        ]
    return blocks[0]


def pack_kernel(count_in, seg_in, fetch_in, params_in, out, count, seg, short, fetch, params, sems):
    segs, span = seg.shape
    nparam, owned = params.shape
    chunks, halves = owned // LANES, span // LANES
    lane = iota((1, LANES), 1)
    pairs = ((params_in, params), (seg_in, seg), (fetch_in, short), (count_in, count))
    copies = [pltpu.make_async_copy(a, b, sems.at[i]) for i, (a, b) in enumerate(pairs)]
    for copy in copies:
        copy.start()
    for copy in copies:
        copy.wait()
    for p in range(nparam):
        for c in range(chunks):
            out[p * chunks + c : p * chunks + c + 1, :] = params[p : p + 1, c * LANES : (c + 1) * LANES]
    at = nparam * chunks
    for s in range(segs):
        for h in range(halves):
            row = jnp.where(lane + h * LANES < count[s], seg[s : s + 1, h * LANES : (h + 1) * LANES], -1)
            out[at : at + 1, :] = row.astype(F32)
            at += 1
    ndev = fetch_in.shape[1]
    rows = SUB * ndev // LANES
    if ndev == LANES:
        out[at : at + SUB, :] = short[...].astype(F32)
        return
    fetch[...] = jnp.zeros(fetch.shape, F32)
    fetch[:, :ndev] = short[...].astype(F32)
    lane, sub = iota((SUB, LANES), 1), iota((SUB, LANES), 0)
    wide = pick(fetch[...], lane & (ndev - 1))
    for r in range(rows):
        own = jnp.where(sub == r * (SUB // rows) + lane // ndev, wide, 0.0)
        out[at + r : at + r + 1, :] = jnp.sum(own, 0, keepdims=True)


def layout_kernel(me_ref, perm, target, tri, goal, goal_cols, back):
    width = back.shape[1]
    ndev = width // 4
    lane = iota((SUB, LANES), 1)
    row = iota((KSEG * width, LANES), 0)
    wanted = ((row & (width - 1)) >> 2) * KSEG + row // width
    for part in range(width // LANES):
        cols = lane + part * LANES
        requester = offset_at(ndev, cols >> 2) ^ me_ref[0]
        same_k = (iota((KSEG * width, LANES), 1) & 3) == (row & 3)
        hit = jnp.zeros((KSEG * width, LANES), F32)
        for s in range(KSEG):
            at = requester * KSEG + s
            held = jnp.zeros((SUB, LANES), F32)
            for g in range(perm.shape[0]):
                source = jnp.broadcast_to(perm[g : g + 1, :].astype(F32), (SUB, LANES))
                held = jnp.where(at >> 7 == g, pick(source, at & (LANES - 1)), held)
            held = held[:1, :].astype(jnp.int32)
            hit = hit + jnp.where((wanted == held) & same_k, 1.0, 0.0)
        back[:, part * LANES : (part + 1) * LANES] = hit.astype(BF16)
    span = tri.shape[2]
    src, dst = iota((span, span), 0), iota((span, span), 1)
    before = (src < dst).astype(F32).astype(BF16)
    after = (src > dst).astype(F32).astype(BF16)
    for half in range(2):
        tri[0, half * span : (half + 1) * span, :] = before
        tri[1, half * span : (half + 1) * span, :] = after
    rows = jnp.concatenate([target[c] for c in range(3)], 0)
    pixels = rows.shape[1]
    wide = jnp.concatenate([rows] * 3 + [jnp.zeros((LANES - 9, pixels), F32)], 0)
    goal[...] = wide[:ROWS]
    goal_cols[...] = wide.T


def render_kernel(segs, cap, nparam, chunks, ndev, *refs):
    me_ref, perm, tri, goal, goal_cols = refs[:5]
    narr = 2 << stages(ndev)[-2][1]
    arrays = refs[5 : 5 + narr]
    image, grads, asked = refs[5 + narr : 8 + narr]
    (fetched, column, ids, lists, idrows, table, hots, coef, alpha, trans, logs, weights, colours, backs, dys, dpar, gback, flat) = refs[8 + narr :]
    main, tail = nparam * chunks + SUB, SUB * ndev // LANES
    unit = 4 * (main + tail)
    per = arrays[0].shape[0] * 4 // unit
    slots = ndev * cap
    quarter = slots // 2
    pixels = SIDE * SIDE
    span = hots.shape[1]
    halves = span // LANES
    me = me_ref[0]
    base = nparam * chunks

    def block(j):
        return arrays[j // per], j % per // 4 * unit + j % 4 * main

    for j in range(ndev):
        ref, at = block(j)
        idrows[j, :SUB, :] = ref[at + base : at + base + SUB, :]
        at = j % per // 4 * unit + 4 * main + j % 4 * tail
        idrows[j, SUB : SUB + tail, :] = ref[at : at + tail, :]
    places = (iota(perm.shape, 0) * LANES + iota(perm.shape, 1)).astype(F32)
    for q in range(KSEG):
        slot = jnp.sum(jnp.where(perm[...] == me * KSEG + q, places, 0.0)).astype(jnp.int32)
        j = position(ndev, (slot >> 2) ^ me)
        fetched[q * tail : (q + 1) * tail, :] = idrows[j, SUB : SUB + tail, :]
        for h in range(halves):
            lists[q * halves + h : q * halves + h + 1, :] = idrows[j, pl.ds((slot & 3) * halves + h, 1), :]
    sub, lane = iota((SUB, LANES), 0), iota((SUB, LANES), 1)
    low_bits = cap.bit_length() - 1
    rank, which = (lane >> low_bits) & (KSEG - 1), lane >> (low_bits + 2)
    kth, share = lane & (cap - 1), SUB // tail
    asked_row = rank * tail + kth // share
    extra = []
    for g in range(ndev // 4):
        offs = [offset_at(ndev, 4 * g + b) for b in range(4)]
        off = jnp.where(which == 0, offs[0], jnp.where(which == 1, offs[1], jnp.where(which == 2, offs[2], offs[3])))
        owner = off ^ me
        found = jnp.zeros((SUB, LANES), F32)
        source = (kth & (share - 1)) * ndev + owner
        for i in range(KSEG * tail // SUB):
            here = pick(fetched[i * SUB : (i + 1) * SUB, :], source)
            found = jnp.where(asked_row == i * SUB + sub, here, found)
        for step in (4, 2, 1):
            found = found + pltpu.roll(found, step, 0)
        local = found.astype(jnp.int32)
        inside, chunk = local & (LANES - 1), local >> 7
        got = []
        for p in range(nparam):
            value = jnp.zeros((SUB, LANES), F32)
            for b in range(4):
                ref, at = block(4 * g + b)
                value = jnp.where(which == b, pick(ref[at + p * chunks : at + (p + 1) * chunks, :], inside), value)
            got.append(jnp.where(sub == chunk, value, 0.0))
        table[g] = sum_rows(got[:SUB])
        last = got[SUB]
        for step in (4, 2, 1):
            last = last + pltpu.roll(last, step, 0)
        extra.append(last)
    listed = lists[...].astype(jnp.int32)
    slot = jnp.maximum(listed, 0)
    pos = position(ndev, (slot >> low_bits) ^ me)
    spot = ((pos & 3) << (low_bits + 2)) + ((sub // halves) << low_bits) + (slot & (cap - 1))
    team = pos >> 2
    live = listed >= 0
    ninth = jnp.zeros((SUB, LANES), F32)
    for g in range(ndev // 4):
        ninth = jnp.where(team == g, pick(extra[g], spot), ninth)
    ninth = jnp.where(live, ninth, 0.0)
    k = slot & (cap - 1)
    into = jnp.where(live, (k >> 2) * quarter + (slot >> low_bits) * 4 + (k & 3), -1).astype(F32)
    for q in range(KSEG):
        for h in range(halves):
            row = q * halves + h
            cols = slice(h * LANES, (h + 1) * LANES)
            spot_row = jnp.broadcast_to(spot[row : row + 1, :], (SUB, LANES))
            team_row = jnp.broadcast_to(team[row : row + 1, :], (SUB, LANES))
            value = jnp.zeros((SUB, LANES), F32)
            for g in range(ndev // 4):
                value = jnp.where(team_row == g, pick(table[g], spot_row), value)
            coef[q, :SUB, cols] = jnp.where(live[row : row + 1, :], value, 0.0)
            coef[q, SUB : SUB + 1, cols] = ninth[row : row + 1, :]
            ids[q : q + 1, cols] = into[row : row + 1, :]
    thin = iota((span, LANES), 1)
    gap = jnp.zeros((ROWS - 9, span), F32)
    groups = []
    for q in range(KSEG):
        hi, mid = split2(coef[q, 6:9, :])
        groups += [hi.astype(F32)] * 3 + [gap] + [mid.astype(F32)] * 3 + [gap]
    columns = jnp.concatenate(groups, 0).T
    for q in range(KSEG):
        both = pltpu.roll(columns, LANES - 2 * q * ROWS, 1) if q else columns
        colours[2 * q * span : (2 * q + 1) * span, :] = jnp.where(thin < 2 * ROWS, both, 0.0).astype(BF16)
        colours[(2 * q + 1) * span : 2 * (q + 1) * span, :] = jnp.where(thin < ROWS, both, 0.0).astype(BF16)
    slot_lane = iota((span, slots), 1)
    fine = (iota((SIDE, span), 0).astype(F32) + 0.5) / SIDE
    pos_x = (me % TILES_X).astype(F32) + fine
    pos_y = (me // TILES_X).astype(F32) + fine

    par, dxs = [], []
    for q in range(KSEG):
        alive = (ids[q : q + 1, :] >= 0.0).astype(F32)
        got = coef[q]
        mx, my = got[0:1], got[1:2]
        ex, ey = jnp.exp(got[2:3]), jnp.exp(got[3:4])
        th = jnp.tanh(got[4:5])
        sa, sc, cross = ex * ex, ey * ey, 0.8 * th * ex * ey
        peak = 0.95 / (1.0 + jnp.exp(-got[5:6])) * alive
        dx = pos_x - mx
        dy = pos_y - my
        xa = -0.5 * sa * dx * dx
        xb = -cross * dx
        dys[q, 0] = dy
        dys[q, 1] = -0.5 * sc * dy * dy
        par.append((sa, sc, cross, ex, ey, th))
        dxs.append(dx)
        for y in range(SIDE):
            power = xa + dys[q, 0, y : y + 1, :] * xb + dys[q, 1, y : y + 1, :]
            al = peak * jnp.exp(power)
            at = slice(y * SIDE, (y + 1) * SIDE)
            alpha[q, at, :] = al
            hi, mid = split2(jnp.log(1.0 - al))
            logs[q, at, :span] = hi
            logs[q, at, span:] = mid
        trans[q] = dot(logs[q], tri[0])

    rows_of = ids[...].T.astype(jnp.int32)
    for q in range(KSEG):
        hots[q] = (slot_lane == rows_of[:, q : q + 1]).astype(F32).astype(BF16)
    ahead = jnp.zeros((pixels, 1), F32)
    lane = iota((pixels, LANES), 1)
    for q in range(KSEG):
        gback[...] = jnp.broadcast_to(ahead, (pixels, LANES))
        ahead = ahead + trans[q, :, span - 1 : span] + jnp.log(1.0 - alpha[q, :, span - 1 : span])
        for y in range(SIDE):
            at = slice(y * SIDE, (y + 1) * SIDE)
            both = jnp.concatenate([gback[at, :]] * halves, 1)
            t = jnp.exp(trans[q, at, :] + both)
            trans[q, at, :] = t
            hi, mid = split2(t * alpha[q, at, :])
            weights[at, 2 * q * span : (2 * q + 1) * span] = hi
            weights[at, (2 * q + 1) * span : 2 * (q + 1) * span] = mid
    shown = dot(weights[...], colours[...])
    e_hi, e_mid = split2(shown - goal_cols[...])
    e_cols = jnp.where((lane < 6) | (lane >= 9), e_hi.astype(F32), e_mid.astype(F32)).astype(BF16)
    shot = shown.T
    shot = shot[:ROWS] + shot[ROWS : 2 * ROWS]
    for c in range(3):
        image[c] = shot[c : c + 1, :]
    er_both = jnp.concatenate(split2(shot - goal[...]), 0)
    for j in range(ndev):
        for k in range(cap):
            row = k // 4 * quarter + 4 * j + k % 4
            column[row : row + 1, :] = idrows[j, SUB + k // share : SUB + k // share + 1, :]
    line = iota(column.shape, 0)
    spot_k = jnp.where(line < quarter, 0, 4) + (line & 3)
    mine = iota(column.shape, 1) == (spot_k & (share - 1)) * ndev + me
    wanted = jnp.sum(jnp.where(mine, column[...], 0.0), 1, keepdims=True).astype(jnp.int32)
    for c in range(chunks):
        cols = iota(column.shape, 1) + c * LANES
        asked[:, c * LANES : (c + 1) * LANES] = (wanted == cols).astype(F32).astype(BF16)
    behind = jnp.zeros((pixels, 1), F32)
    for q in range(KSEG):
        hi, mid = split2(coef[q, 6:9, :])
        hi, mid = hi.astype(F32), mid.astype(F32)
        gap = jnp.zeros((ROWS - 9, span), F32)
        c_rows = jnp.concatenate([hi, mid, hi, gap, hi, jnp.zeros((LANES - ROWS - 3, span), F32)], 0).astype(BF16)
        slope = dot(e_cols, c_rows)
        dcol = dot(er_both, weights[:, 2 * q * span : (2 * q + 1) * span])
        dcol = dcol[:ROWS] + dcol[ROWS:] + dot(er_both[:ROWS], weights[:, (2 * q + 1) * span : 2 * (q + 1) * span])
        dpar[q, 6:9, :] = dcol[0:3]
        for y in range(SIDE):
            at = slice(y * SIDE, (y + 1) * SIDE)
            gt = slope[at] * trans[q, at, :]
            trans[q, at, :] = gt
            hi, mid = split2(gt * alpha[q, at, :])
            logs[q, at, :span] = hi
            logs[q, at, span:] = mid
        backs[q] = dot(logs[q], tri[1])
    for q in reversed(range(KSEG)):
        gback[...] = jnp.broadcast_to(behind, (pixels, LANES))
        behind = behind + backs[q, :, 0:1] + trans[q, :, 0:1] * alpha[q, :, 0:1]
        sa, sc, cross, ex, ey, th = par[q]
        dx = dxs[q]
        d0 = jnp.zeros((SIDE, span), F32)
        d1 = jnp.zeros((SIDE, span), F32)
        d2 = jnp.zeros((SIDE, span), F32)
        for y in range(SIDE):
            at = slice(y * SIDE, (y + 1) * SIDE)
            both = jnp.concatenate([gback[at, :]] * halves, 1)
            al = alpha[q, at, :]
            d = (trans[q, at, :] - (backs[q, at, :] + both) / (1.0 - al)) * al
            ddy = d * dys[q, 0, y : y + 1, :]
            d0 = d0 + d
            d1 = d1 + ddy
            d2 = d2 + ddy * dys[q, 0, y : y + 1, :]
        m0 = jnp.sum(d0, 0, keepdims=True)
        m_x = jnp.sum(d0 * dx, 0, keepdims=True)
        m_y = jnp.sum(d1, 0, keepdims=True)
        m_xx = jnp.sum(d0 * dx * dx, 0, keepdims=True)
        m_xy = jnp.sum(d1 * dx, 0, keepdims=True)
        m_yy = jnp.sum(d2, 0, keepdims=True)
        dpar[q, 0:1, :] = sa * m_x + cross * m_y
        dpar[q, 1:2, :] = cross * m_x + sc * m_y
        dpar[q, 2:3, :] = -(sa * m_xx + cross * m_xy)
        dpar[q, 3:4, :] = -(sc * m_yy + cross * m_xy)
        dpar[q, 4:5, :] = -0.8 * (1.0 - th) * (1.0 + th) * ex * ey * m_xy
        dpar[q, 5:6, :] = m0 / (1.0 + jnp.exp(coef[q, 5:6, :]))
        dpar[q, nparam:, :] = jnp.zeros((ROWS - nparam, span), F32)
        parts = jnp.concatenate(split3(dpar[q]), 0)
        back = dot(parts, hots[q])
        back = back[:ROWS] + back[ROWS : 2 * ROWS] + back[2 * ROWS :]
        for half in range(2):
            row = half * KSEG * ROWS + q * ROWS
            flat[row : row + ROWS, :] = back[:, half * quarter : (half + 1) * quarter]
    turned = flat[...].T
    for o in range(ndev):
        grads[o] = turned[4 * o : 4 * o + 4, :]


def update_kernel(returned, back, hot, params, moment, second, new_params, new_moment, new_second):
    nparam = params.shape[0]
    flat = returned[...].T
    half = KSEG * ROWS
    sides = [
        jnp.concatenate([flat[h * half + q * ROWS : h * half + (q + 1) * ROWS] for q in range(KSEG)], 1)
        for h in range(2)
    ]
    parts = jnp.concatenate(split3(jnp.concatenate(sides, 0)), 0)
    asked = dot(parts, back[...])
    asked = asked[: 2 * ROWS] + asked[2 * ROWS : 4 * ROWS] + asked[4 * ROWS :]
    parts = jnp.concatenate(split3(jnp.concatenate([asked[:ROWS], asked[ROWS:]], 1)), 0)
    grad = dot(parts, hot[...])
    grad = (grad[:ROWS] + grad[ROWS : 2 * ROWS] + grad[2 * ROWS :])[:nparam]
    m = 0.9 * moment[...] + 0.1 * grad
    v = 0.99 * second[...] + 0.01 * grad * grad
    new_moment[...] = m
    new_second[...] = v
    new_params[...] = params[...] - 0.05 * m / (jnp.sqrt(v) + 1e-08)


def per_device(params, moment, second, fetch_ids, seg_ids, seg_count, seg_perm, target):
    ndev = lax.axis_size("dev")
    nparam, owned = params.shape
    segs, span = seg_ids.shape
    cap = fetch_ids.shape[2]
    pixels = target.shape[2]
    slots = ndev * cap
    chunks = owned // LANES
    lists = segs * span // LANES
    assert target.shape[0] == 1 and segs == KSEG and pixels == SIDE * SIDE
    assert cap == SUB and chunks == SUB and lists == SUB and ndev <= LANES and nparam == SUB + 1
    base = nparam * chunks
    perm = seg_perm.reshape(-1, LANES)
    me = lax.axis_index("dev").astype(jnp.int32).reshape(1)

    in_hbm = functools.partial(pltpu.with_memory_space_constraint, memory_space=pltpu.HBM)

    packed = pl.pallas_call(
        pack_kernel,
        out_shape=jax.ShapeDtypeStruct((base + SUB + slots // LANES, LANES), F32),
        in_specs=[HBM] * 4,
        out_specs=VMEM,
        scratch_shapes=[
            pltpu.SMEM(seg_count.shape, jnp.int32),
            pltpu.VMEM(seg_ids.shape, jnp.int32),
            pltpu.VMEM((cap, ndev), jnp.int32),
            pltpu.VMEM((cap, LANES), F32),
            pltpu.VMEM(params.shape, F32),
            pltpu.SemaphoreType.DMA((4,)),
        ],
        compiler_params=PARAMS,
        name="pack",
    )(*[in_hbm(x) for x in (seg_count, seg_ids, fetch_ids[0].T, params)])
    tri, goal, goal_cols, back = pl.pallas_call(
        layout_kernel,
        out_shape=(
            jax.ShapeDtypeStruct((2, 2 * span, span), BF16),
            jax.ShapeDtypeStruct((ROWS, pixels), F32),
            jax.ShapeDtypeStruct((pixels, LANES), F32),
            jax.ShapeDtypeStruct((KSEG * 4 * ndev, 4 * ndev), BF16),
        ),
        in_specs=[SMEM, VMEM, VMEM],
        out_specs=(VMEM, VMEM, VMEM, VMEM),
        compiler_params=PARAMS,
        cost_estimate=pl.CostEstimate(flops=0, bytes_accessed=4 * 2**20, transcendentals=0),
        name="layout",
    )(me, perm, target.transpose(1, 0, 2))
    blocks, (tri, goal, goal_cols, back) = gather_blocks(packed, ndev, base + SUB, (tri, goal, goal_cols, back))
    image, grads, hot = pl.pallas_call(
        functools.partial(render_kernel, segs, cap, nparam, chunks, ndev),
        out_shape=(
            jax.ShapeDtypeStruct((3, 1, pixels), F32),
            jax.ShapeDtypeStruct((ndev, 4, LANES), F32),
            jax.ShapeDtypeStruct((slots, owned), BF16),
        ),
        in_specs=[SMEM] + [VMEM] * (4 + len(blocks)),
        out_specs=(VMEM, VMEM, VMEM),
        scratch_shapes=[
            pltpu.VMEM((KSEG * SUB * ndev // LANES, LANES), F32),
            pltpu.VMEM((slots, LANES), F32),
            pltpu.VMEM((SUB, span), F32),
            pltpu.VMEM((SUB, LANES), F32),
            pltpu.VMEM((ndev, 2 * SUB, LANES), F32),
            pltpu.VMEM((ndev // 4, SUB, LANES), F32),
            pltpu.VMEM((KSEG, span, slots), BF16),
            pltpu.VMEM((KSEG, ROWS, span), F32),
            pltpu.VMEM((KSEG, pixels, span), F32),
            pltpu.VMEM((KSEG, pixels, span), F32),
            pltpu.VMEM((KSEG, pixels, 2 * span), BF16),
            pltpu.VMEM((pixels, 2 * KSEG * span), BF16),
            pltpu.VMEM((2 * KSEG * span, LANES), BF16),
            pltpu.VMEM((KSEG, pixels, span), F32),
            pltpu.VMEM((KSEG, 2, SIDE, span), F32),
            pltpu.VMEM((KSEG, ROWS, span), F32),
            pltpu.VMEM((pixels, LANES), F32),
            pltpu.VMEM((LANES, slots // 2), F32),
        ],
        compiler_params=PARAMS,
        name="render",
    )(me, perm, tri, goal, goal_cols, *blocks)
    returned = lax.all_to_all(grads, "dev", split_axis=0, concat_axis=0, tiled=True)
    new = jax.ShapeDtypeStruct(params.shape, F32)
    new_params, new_moment, new_second = pl.pallas_call(
        update_kernel,
        out_shape=(new, new, new),
        in_specs=[VMEM] * 6,
        out_specs=(VMEM, VMEM, VMEM),
        compiler_params=PARAMS,
        name="update",
    )(returned.reshape(4 * ndev, LANES), back, hot, params, moment, second)
    return (image.transpose(1, 0, 2), new_params, new_moment, new_second)


def solution(mesh):
    placed = (
        P(None, "dev"),
        P(None, "dev"),
        P(None, "dev"),
        P("dev", None, None),
        P("dev", None),
        P("dev"),
        P(),
        P("dev", None, None),
    )
    return jax.shard_map(
        per_device,
        mesh=mesh,
        in_specs=placed,
        out_specs=(P("dev", None, None), P(None, "dev"), P(None, "dev"), P(None, "dev")),
        check_vma=False,
    )
```
